128 devices in a mesh: member: 16 (over z, y_lo, core), band: 8 (over x, y_hi).
Axes of the slice: x: 4, y: 4 (y_hi: 2, y_lo: 2; y = y_hi * 2 + y_lo), z: 4, core: 2. Of those that a mesh axis runs over, the one named last changes fastest.
Arguments:
- states: bfloat16 [32, 84, 128, 128], P('member', None, 'band'), may hold values from -6 to 6
- noise_field: float32 [32, 84, 128, 128], P('member', None, 'band'), may hold values from -3 to 3
- target: bfloat16 [84, 128, 128], P(None, 'band'), may hold values from -6 to 6
- w_conv: bfloat16 [512, 756], replicated, may hold values from -0.21875 to 0.21875
- w_proj: bfloat16 [84, 512], replicated, may hold values from -0.25 to 0.25
- matchings: int32 [4, 32], replicated, may hold values from 0 to 31, each once within a row
Outputs:
- grad_states: bfloat16 [32, 84, 128, 128], P('member', None, 'band')
- grad_conv: float32 [512, 756], P(('member', 'band'))
- grad_proj: float32 [84, 512], P(None, ('member', 'band'))
The draws below stay inside these ranges and needn't reach their ends.
Inputs may be any that keep to these rules, and one draw needn't show every extreme that they name: `matchings`: each row is a permutation of the 32 member numbers.
All inputs are finite; a program needn't handle non-finite values.
Results may differ from the reference program's by a relative error of at most 0.0075.
Values may be sent and summed in bfloat16 or wider, within the bound.
A program may use at most 128 MiB of HBM per device.

```python
import math
import jax
import jax.numpy as jnp
from jax import lax

VARS = 84
HID = 512
MATCHES = 4
LON = 128
MEMBERS = 32
LAT = 128


def levels(rng, dims, cuts, smallest, high):
    gain, own = 1.0, jax.random.fold_in(rng, 6)
    for dim, shards_of in cuts:
        draws = jnp.exp(jax.random.uniform(jax.random.fold_in(own, dim), (shards_of,), jnp.float32, smallest / len(cuts), high / len(cuts)))
        gain = gain * jnp.repeat(draws, dims[dim] // shards_of).reshape([-1 if axis == dim else 1 for axis in range(len(dims))])
    return gain


def bell_draw(key, dims, deviation, limit, split=(), kind=jnp.bfloat16):
    result = deviation * jax.random.normal(key, dims, jnp.float32)
    if split:
        result = result * levels(key, dims, split, -0.22, 0.18)
    return jnp.clip(result, -limit, limit).astype(kind)


def setup_inputs(seed: int = 0) -> dict:
    splits = jax.random.split(jax.random.key(seed), 7)
    states = bell_draw(splits[0], (MEMBERS, VARS, LAT, LON), 1.0, 6.0, ((0, 16), (2, 8)))
    noise_field = bell_draw(splits[1], (MEMBERS, VARS, LAT, LON), 0.5, 3.0, ((0, 16), (2, 8)), jnp.float32)
    target = bell_draw(splits[2], (VARS, LAT, LON), 1.0, 6.0, ((1, 8),))
    w_conv = bell_draw(splits[3], (HID, 9 * VARS), (9 * VARS) ** -0.5, 0.21875)
    w_proj = bell_draw(splits[4], (VARS, HID), HID ** -0.5, 0.25)
    matchings = jax.vmap(lambda own: jax.random.permutation(own, MEMBERS))(jax.random.split(splits[5], MATCHES)).reshape((MATCHES, MEMBERS)).astype(jnp.int32)
    return dict(states=states, noise_field=noise_field, target=target, w_conv=w_conv, w_proj=w_proj, matchings=matchings)


SQRT_HALF = 0.7071067811865476
INV_ROOT_TWO_PI = 0.3989422804014327

def gelu_slope(preact):
    return 0.5 * (1.0 + lax.erf(preact * SQRT_HALF)) + preact * jnp.exp(-0.5 * preact * preact) * INV_ROOT_TWO_PI

def to_patches(values_in):
    leading = values_in.shape[:-3]
    channels, height, breadth = values_in.shape[-3:]
    n_lead = len(leading)
    blocks = values_in.reshape(leading + (channels, height // 8, 8, breadth // 4, 4))
    order = tuple(range(n_lead)) + (n_lead + 1, n_lead + 3, n_lead, n_lead + 2, n_lead + 4)
    blocks = jnp.transpose(blocks, order)
    return blocks.reshape(leading + (height // 8 * (breadth // 4), channels * 32))

def from_patches(values_in, channels, height, breadth):
    leading = values_in.shape[:-2]
    n_lead = len(leading)
    blocks = values_in.reshape(leading + (height // 8, breadth // 4, channels, 8, 4))
    order = tuple(range(n_lead)) + (n_lead + 2, n_lead, n_lead + 3, n_lead + 1, n_lead + 4)
    return jnp.transpose(blocks, order).reshape(leading + (channels, height, breadth))

def score_grad(differ):
    return differ * lax.rsqrt(lax.optimization_barrier(jnp.mean(differ * differ, axis=-1, keepdims=True)) + 1e-06)

def unfold(inputs_bf):
    channels, height, breadth = inputs_bf.shape
    padded = jnp.pad(inputs_bf, ((0, 0), (1, 1), (1, 1)))
    pieces = [padded[:, row_off:row_off + height, col_off:col_off + breadth] for row_off in range(3) for col_off in range(3)]
    return jnp.stack(pieces, axis=0).reshape(9 * channels, height * breadth)

def fold_back(grads):
    channels, height, breadth = grads.shape[1:]
    summed = jnp.zeros((channels, height + 2, breadth + 2), jnp.float32)
    for row_off in range(3):
        for col_off in range(3):
            summed = summed.at[:, row_off:row_off + height, col_off:col_off + breadth].add(grads[row_off * 3 + col_off])
    return summed[:, 1:-1, 1:-1]

def reference(states, noise_field, target, w_conv, w_proj, matchings):
    channels, height, breadth = states.shape[1:]
    count = matchings.shape[0]

    def prepare(states_m, noise_m):
        inputs_bf = (states_m.astype(jnp.float32) + noise_m).astype(jnp.bfloat16)
        columns = unfold(inputs_bf)
        preact = jnp.dot(w_conv, columns, preferred_element_type=jnp.float32)
        hidden = jax.nn.gelu(preact, approximate=False).astype(jnp.bfloat16)
        return (inputs_bf, columns, preact, hidden)

    def forward(item):
        inputs_bf, columns, preact, hidden = prepare(item[0], item[1])
        outputs = inputs_bf.astype(jnp.float32).reshape(channels, -1) + jnp.dot(w_proj, hidden, preferred_element_type=jnp.float32)
        return outputs.astype(jnp.bfloat16).reshape(channels, height, breadth)
    predicted = lax.map(forward, (states, noise_field))
    patches_all = to_patches(predicted)
    target_p = to_patches(target).astype(jnp.float32)
    numbers = jnp.broadcast_to(jnp.arange(MEMBERS, dtype=jnp.int32)[None, :], matchings.shape)
    inverse = jnp.zeros_like(matchings).at[jnp.arange(count, dtype=jnp.int32)[:, None], matchings].set(numbers)

    def member_grad(member):
        own_vals = patches_all[member].astype(jnp.float32)
        total = score_grad(own_vals - target_p)
        pair_sum = jnp.zeros_like(own_vals)
        for match in range(count):
            for lookup in (matchings, inverse):
                pair_sum = pair_sum + score_grad(own_vals - patches_all[lookup[match, member]].astype(jnp.float32))
        return (total - pair_sum / (2.0 * count)).astype(jnp.bfloat16)
    grads_p = lax.map(member_grad, jnp.arange(MEMBERS, dtype=jnp.int32))
    grad_pred = from_patches(grads_p, channels, height, breadth)

    def backward(carry, item):
        inputs_bf, columns, preact, hidden = prepare(item[0], item[1])
        grad_flat = item[2].reshape(channels, -1)
        dhidden = jnp.dot(w_proj.T, grad_flat, preferred_element_type=jnp.float32)
        grad_pre = (dhidden * gelu_slope(preact)).astype(jnp.bfloat16)
        conv_acc = carry[0] + jnp.dot(grad_pre, columns.T, preferred_element_type=jnp.float32)
        proj_acc = carry[1] + jnp.dot(grad_flat, hidden.T, preferred_element_type=jnp.float32)
        dcolumns = jnp.dot(w_conv.T, grad_pre, preferred_element_type=jnp.float32).reshape(9, channels, height, breadth)
        dinput = grad_flat.astype(jnp.float32).reshape(channels, height, breadth) + fold_back(dcolumns)
        return ((conv_acc, proj_acc), dinput.astype(jnp.bfloat16))
    start = (jnp.zeros(w_conv.shape, jnp.float32), jnp.zeros(w_proj.shape, jnp.float32))
    totals, grad_states = lax.scan(backward, start, (states, noise_field, grad_pred))
    factor = 1.0 / math.sqrt(MEMBERS * LAT * LON)
    return (grad_states, totals[0] * factor, totals[1] * factor)
```

```python
import functools

import jax
import jax.numpy as jnp
import ml_dtypes
import numpy as np
from jax import lax
from jax.experimental import pallas as pl
from jax.experimental.pallas import tpu as pltpu
from jax.sharding import PartitionSpec as P

F32, BF16 = jnp.float32, jnp.bfloat16
MESH = pl.DeviceIdType.MESH
V, VP, VQ = 84, 96, 88
R, C, H = 16, 128, 512
NM, NB, NK = 16, 8, 4
MEMBERS = 2 * NM
KP = 256
ORDER = (
    [co * V + v for co in range(3) for v in range(80)]
    + [co * V + v for co in range(3) for v in range(80, V)]
)
CHUNKS = (384, 256, 256)


def selection():
    table = np.zeros((9 * V, 3 * KP), ml_dtypes.bfloat16)
    for ro in range(3):
        for place, source in enumerate(ORDER):
            table[ro * 3 * V + source, ro * KP + place] = 1
    return table


def patch_order():
    table = np.zeros((8 * C, 8 * C), ml_dtypes.bfloat16)
    for row in range(8):
        for lon in range(C):
            group, patch, col = lon // 16, lon % 16 // 4, lon % 4
            table[row * C + lon, group * 128 + (row * 4 + col) * 4 + patch] = 1
    return table


def remote(src, dst, send_sem, recv_sem, **device):
    return pltpu.make_async_remote_copy(
        src_ref=src, dst_ref=dst, send_sem=send_sem, recv_sem=recv_sem,
        device_id=device, device_id_type=MESH,
    )


def gelu_and_slope(x):
    e = jnp.exp(-0.5 * x * x)
    t = 1.0 / (1.0 + (0.3275911 * 0.7071067811865476) * jnp.abs(x))
    poly = 1.061405429 * 0.5
    for coef in (-1.453152027, 1.421413741, -0.284496736, 0.254829592):
        poly = poly * t + 0.5 * coef
    tail = poly * t * e
    phi = jnp.where(x >= 0.0, 1.0 - tail, tail)
    return x * phi, phi + x * e * 0.3989422804014327


def dot(a, b):
    return jnp.dot(a, b, preferred_element_type=F32)


def dot_nt(a, b):
    return lax.dot_general(a, b, (((1,), (1,)), ((), ())), preferred_element_type=F32)


def kernel(
    states, noise, target, w_conv, w_proj, select, perm, match, inverse,
    out, sums,
    xf, x3, hs, hb, wf, wt, wp, wpt, hidden, slope, pn, sb, rb, pf, tf, tp, es, sc, gb, gr, gn, gp, of,
    hsb, hrb, a0, a1, a2, s10, s11, s12, r10, r11, r12, s20, s21, s22, r20, r21, r22, s3, r3,
    h_send, h_recv, p_send, p_recv, g_send, g_recv, o_send, o_recv,
    u_send, u_recv, v_send, v_recv, w_send, w_recv,
):
    me, band = lax.axis_index("member"), lax.axis_index("band")
    core, chip = lax.rem(me, 2), lax.div(me, 2)
    lanes = lax.broadcasted_iota(jnp.int32, (VP, C), 1)
    acc = (a0, a1, a2)
    s1, r1, s2, r2 = (s10, s11, s12), (r10, r11, r12), (s20, s21, s22), (r20, r21, r22)

    barrier = pltpu.get_barrier_semaphore()

    def greet_member(step, _):
        pl.semaphore_signal(barrier, inc=1, device_id={"member": lax.rem(me + step, NM)}, device_id_type=MESH)
        return 0

    def greet_band(step, _):
        pl.semaphore_signal(barrier, inc=1, device_id={"band": lax.rem(band + step, NB)}, device_id_type=MESH)
        return 0

    lax.fori_loop(1, NM, greet_member, 0)
    lax.fori_loop(1, NB, greet_band, 0)

    def add_inputs(c, _):
        part = pl.ds(c * 12, 12)
        to = pl.ds(pl.multiple_of(c * 192, 192), 192)
        for m in range(2):
            value = (states[m, part].astype(F32) + noise[m, part]).astype(BF16).astype(F32)
            xf[m, to, :] = value.reshape(192, C)
        tf[to, :] = target[part].astype(F32).reshape(192, C)
        return 0

    lax.fori_loop(0, V // 12, add_inputs, 0)
    for m in range(2):
        xf[m, V * R:, :] = jnp.zeros(((VP - V) * R, C), F32)
    tf[V * R:, :] = jnp.zeros(((VP - V) * R, C), F32)

    for side, row in ((0, 0), (1, R - 1)):
        for m in range(2):
            hs[side, m] = xf[m, pl.ds(row, VP, stride=R), :].astype(BF16)

    pl.semaphore_wait(barrier, NM + NB - 2)
    def halo(side):
        to = band - 1 if side == 0 else band + 1
        return remote(hs.at[side], hb.at[1 - side], h_send.at[side], h_recv.at[1 - side], band=to)

    pl.when(band > 0)(lambda: halo(0).start())
    pl.when(band < NB - 1)(lambda: halo(1).start())

    def put_row(m, slot, x):
        left = jnp.where(lanes == 0, 0.0, pltpu.roll(x, 1, 1))
        right = jnp.where(lanes == C - 1, 0.0, pltpu.roll(x, C - 1, 1))
        x3[m, slot, 0:80, :] = left[0:80].astype(BF16)
        x3[m, slot, 80:160, :] = x[0:80].astype(BF16)
        x3[m, slot, 160:240, :] = right[0:80].astype(BF16)
        first = left[80:88] + pltpu.roll(x[80:88], 4, 0)
        x3[m, slot, 240:256, :] = jnp.concatenate([first, right[80:88]], axis=0).astype(BF16)

    def build(r, _):
        for m in range(2):
            put_row(m, r + 1, xf[m, pl.ds(r, VP, stride=R), :])
        return 0

    lax.fori_loop(0, R, build, 0)

    for ro in range(3):
        w_part = dot(w_conv[...], select[:, ro * KP:(ro + 1) * KP])
        wf[:, ro * KP:(ro + 1) * KP] = w_part.astype(BF16)
        wt[:, ro * H:(ro + 1) * H] = w_part.T.astype(BF16)
    w_pad = jnp.concatenate([w_proj[...].astype(F32), jnp.zeros((VP - V, H), F32)], axis=0)
    wp[...] = w_pad.astype(BF16)
    wpt[...] = w_pad.T.astype(BF16)

    def halo_in(side, slot):
        remote(hs.at[1 - side], hb.at[side], h_send.at[1 - side], h_recv.at[side], band=band).wait_recv()
        for m in range(2):
            put_row(m, slot, hb[side, m].astype(F32))

    def no_halo(slot):
        for m in range(2):
            x3[m, slot] = jnp.zeros((KP, C), BF16)

    pl.when(band > 0)(lambda: halo_in(0, 0))
    pl.when(band == 0)(lambda: no_halo(0))
    pl.when(band < NB - 1)(lambda: halo_in(1, R + 1))
    pl.when(band == NB - 1)(lambda: no_halo(R + 1))
    pl.when(band > 0)(lambda: halo(0).wait_send())
    pl.when(band < NB - 1)(lambda: halo(1).wait_send())

    def pair(ref, m, i):
        return jnp.concatenate([ref[m, i], ref[m, i + 1]], axis=1)

    def predicted_copy(j, source):
        return remote(sb.at[j], rb.at[source], p_send.at[j], p_recv.at[source], member=j)

    for pr in range(2):
        def forward(rp, _):
            i = pr * 8 + rp * 2
            for m in range(2):
                columns = jnp.concatenate([pair(x3, m, i + ro) for ro in range(3)], axis=0)
                pre = dot(wf[...], columns)
                value, grad = gelu_and_slope(pre)
                value = value.astype(BF16)
                for k in range(2):
                    hidden[m, i + k] = value[:, k * C:(k + 1) * C]
                    slope[m, i + k] = grad[:, k * C:(k + 1) * C]
                own = jnp.concatenate([xf[m, pl.ds(i + k, VP, stride=R), :] for k in range(2)], axis=1)
                pn[rp, m * VP:(m + 1) * VP, :] = (own + dot(wp[...], value)).astype(BF16)
            return 0

        lax.fori_loop(0, 4, forward, 0)
        moved = dot(jnp.concatenate([pn[rp] for rp in range(4)], axis=1), perm[...]).astype(BF16)
        for lg in range(8):
            for m in range(2):
                sb[2 * lg + pr, m] = moved[m * VP:(m + 1) * VP, lg * C:(lg + 1) * C]

        def send(step, _):
            j = 2 * lax.rem(chip + step, NM // 2) + pr

            @pl.when(j != me)
            def _():
                predicted_copy(j, me).start()

            @pl.when(j == me)
            def _():
                rb[me] = sb[me]
            return 0

        lax.fori_loop(1, NM // 2 + 1, send, 0)

    rows = jnp.concatenate(
        [tf[pl.ds(core * 8 + r, VP, stride=R), :] for r in range(8)], axis=1
    ).astype(BF16)
    moved = dot(rows, perm[...])
    for lg in range(8):
        tp[lg] = moved[:, lg * C:(lg + 1) * C]
    gp_zero = jnp.zeros((H, C), BF16)
    for m in range(2):
        gp[m, 0] = gp_zero
        gp[m, R + 1] = gp_zero

    def arrive(source, _):
        @pl.when(source != me)
        def _():
            predicted_copy(source, source).wait_recv()
        for m in range(2):
            pf[source * 2 + m] = rb[source, m].astype(F32)
        return 0

    lax.fori_loop(0, NM, arrive, 0)

    def square(d):
        d = d * d
        total = d[0:8]
        for k in range(1, VQ // 8):
            total = total + d[k * 8:(k + 1) * 8]
        return total

    def edges(m, _):
        own = pf[m, 0:VQ, :]
        es[pl.ds(pl.multiple_of((NK * MEMBERS + m) * 8, 8), 8), :] = square(own - tp[chip, 0:VQ, :])
        for k in range(NK):
            es[pl.ds(pl.multiple_of((k * MEMBERS + m) * 8, 8), 8), :] = square(own - pf[match[k, m], 0:VQ, :])
        return 0

    lax.fori_loop(0, MEMBERS, edges, 0)
    count = (NK + 1) * MEMBERS
    total = es[pl.ds(0, count, stride=8), :]
    for k in range(1, 8):
        total = total + es[pl.ds(k, count, stride=8), :]
    for shift in (4, 8, 16, 32, 64):
        total = total + pltpu.roll(total, shift, 1)
    sc[...] = lax.rsqrt(total / (32.0 * V) + 1e-06)

    def gradient_copy(j, source):
        return remote(gb.at[j], gr.at[source], g_send.at[j], g_recv.at[source], member=j)

    def member_pair(step, _):
        j = lax.rem(me + step, NM)
        for mm in range(2):
            m = j * 2 + mm
            own = pf[m, 0:VQ, :]
            pairs = jnp.zeros((VQ, C), F32)
            for k in range(NK):
                n, n_inv = match[k, m], inverse[k, m]
                pairs = pairs + (own - pf[n, 0:VQ, :]) * sc[pl.ds(k * MEMBERS + m, 1), :]
                pairs = pairs + (own - pf[n_inv, 0:VQ, :]) * sc[pl.ds(k * MEMBERS + n_inv, 1), :]
            truth = (own - tp[chip, 0:VQ, :]) * sc[pl.ds(NK * MEMBERS + m, 1), :]
            grad = truth - pairs * (0.5 / NK)
            gb[j, mm] = jnp.concatenate([grad, jnp.zeros((VP - VQ, C), F32)], axis=0).astype(BF16)

        @pl.when(j != me)
        def _():
            gradient_copy(j, me).start()

        @pl.when(j == me)
        def _():
            gr[me] = gb[me]
        return 0

    lax.fori_loop(1, NM + 1, member_pair, 0)

    def gradients_in(source, _):
        @pl.when(source != me)
        def _():
            gradient_copy(source, source).wait_recv()
        return 0

    lax.fori_loop(0, NM, gradients_in, 0)
    for pr in range(2):
        parts = [jnp.concatenate([gr[2 * lg + pr, 0], gr[2 * lg + pr, 1]], axis=0) for lg in range(8)]
        back = dot_nt(jnp.concatenate(parts, axis=1), perm[...]).astype(BF16)
        for m in range(2):
            for r in range(8):
                gn[m, pr * 8 + r] = back[m * VP:(m + 1) * VP, r * C:(r + 1) * C]

    def hidden_grad(rp, _):
        i = rp * 2
        for m in range(2):
            dh = dot(wpt[...], pair(gn, m, i))
            for k in range(2):
                gp[m, i + k + 1] = (dh[:, k * C:(k + 1) * C] * slope[m, i + k]).astype(BF16)
        return 0

    lax.fori_loop(0, R // 2, hidden_grad, 0)

    def wide(ref, m, i):
        return jnp.concatenate([ref[m, i + k] for k in range(8)], axis=1)

    def conv_term(ro):
        acc[ro][:, 0:KP] = jnp.zeros((H, KP), F32)

        def step(s, _):
            m, i = lax.div(s, 2), lax.rem(s, 2) * 8
            acc[ro][:, 0:KP] += dot_nt(wide(gp, m, i + 1), wide(x3, m, i + ro))
            return 0

        lax.fori_loop(0, 4, step, 0)

    def proj_term():
        acc[0][:, KP:] = jnp.zeros((H, 128), F32)

        def step(s, _):
            m, i = lax.div(s, 2), lax.rem(s, 2) * 8
            acc[0][:, KP:KP + VP] += dot_nt(wide(hidden, m, i), wide(gn, m, i))
            return 0

        lax.fori_loop(0, 4, step, 0)

    def core_copy(q):
        return remote(s1[q], r1[q], u_send.at[q], u_recv.at[q], member=me + 1 - 2 * core)

    def core_send(q):
        for c in range(NM // 2):
            base = c * 64 + (1 - core) * 32
            s1[q][c] = acc[q][pl.ds(pl.multiple_of(base, 32), 32), :].astype(BF16)
        core_copy(q).start()

    def chip_copy(q, c, source):
        return remote(s2[q].at[c], r2[q].at[source], v_send.at[q, c], v_recv.at[q, source], member=2 * c + core)

    def chip_send(q):
        core_copy(q).wait()
        for c in range(NM // 2):
            base = c * 64 + core * 32
            s2[q][c] = (acc[q][pl.ds(pl.multiple_of(base, 32), 32), :] + r1[q][c].astype(F32)).astype(BF16)

        def send(step, _):
            c = lax.rem(chip + step, NM // 2)
            chip_copy(q, c, chip).start()
            return 0

        lax.fori_loop(1, NM // 2, send, 0)

    def chip_sum(q):
        def take(step, total):
            c = lax.rem(chip + step, NM // 2)
            chip_copy(q, c, c).wait_recv()
            chip_copy(q, c, c).wait_send()
            return total + r2[q][c].astype(F32)

        return lax.fori_loop(1, NM // 2, take, s2[q][chip].astype(F32))

    def band_copy(b, source):
        return remote(s3.at[b], r3.at[source], w_send.at[b], w_recv.at[source], band=b)

    proj_term()
    conv_term(0)
    core_send(0)
    conv_term(1)
    core_send(1)
    chip_send(0)
    conv_term(2)
    core_send(2)
    chip_send(1)

    def fold(d):
        def spread(a):
            return (
                jnp.where(lanes[0:a.shape[0]] == C - 1, 0.0, pltpu.roll(a, C - 1, 1)),
                jnp.where(lanes[0:a.shape[0]] == 0, 0.0, pltpu.roll(a, 1, 1)),
            )
        body = spread(d[0:80])[0] + d[80:160] + spread(d[160:240])[1]
        last = spread(d[240:248])[0] + pltpu.roll(d[240:248], 4, 0) + spread(d[248:256])[1]
        return jnp.concatenate([body, last], axis=0)

    for side, ro, row in ((0, 0, 1), (1, 2, R)):
        rows = jnp.concatenate([gp[0, row], gp[1, row]], axis=1)
        d = dot(wt[:, ro * H:(ro + 1) * H], rows)
        for m in range(2):
            hsb[side, m] = fold(d[:, m * C:(m + 1) * C])

    def out_halo(side):
        to = band - 1 if side == 0 else band + 1
        return remote(hsb.at[side], hrb.at[1 - side], o_send.at[side], o_recv.at[1 - side], band=to)

    pl.when(band > 0)(lambda: out_halo(0).start())
    pl.when(band < NB - 1)(lambda: out_halo(1).start())

    def input_grad(m):
        def step(rp, _):
            i = rp * 2
            rows = jnp.concatenate([pair(gp, m, i + 2 - ro) for ro in range(3)], axis=0)
            d = dot(wt[...], rows)
            for k in range(2):
                value = fold(d[:, k * C:(k + 1) * C]) + gn[m, i + k].astype(F32)[0:VQ]
                of[m, pl.ds(i + k, VQ, stride=R), :] = value
            return 0

        lax.fori_loop(0, R // 2, step, 0)

    chip_send(2)
    input_grad(0)
    for q, width, base in ((0, 384, 0), (1, 256, 384), (2, 256, 640)):
        total = chip_sum(q)
        for b in range(NB):
            s3[b, :, base:base + width] = total[b * 4:(b + 1) * 4]

    def band_send(step, _):
        b = lax.rem(band + step, NB)
        band_copy(b, band).start()
        return 0

    lax.fori_loop(1, NB, band_send, 0)
    input_grad(1)

    def out_halo_in(side, row):
        remote(hsb.at[1 - side], hrb.at[side], o_send.at[1 - side], o_recv.at[side], band=band).wait_recv()
        for m in range(2):
            of[m, pl.ds(row, VQ, stride=R), :] += hrb[side, m]

    pl.when(band > 0)(lambda: out_halo_in(0, 0))
    pl.when(band < NB - 1)(lambda: out_halo_in(1, R - 1))

    def write(c, _):
        for m in range(2):
            value = of[m, pl.ds(pl.multiple_of(c * 192, 192), 192), :]
            out[m, pl.ds(c * 12, 12)] = value.reshape(12, R, C).astype(BF16)
        return 0

    lax.fori_loop(0, V // 12, write, 0)

    def band_take(step, total):
        b = lax.rem(band + step, NB)
        band_copy(b, b).wait_recv()
        band_copy(b, b).wait_send()
        return total + r3[b]

    total = lax.fori_loop(1, NB, band_take, s3[band])
    sums[...] = total * (1.0 / (MEMBERS * NB * R * C) ** 0.5)

    pl.when(band > 0)(lambda: out_halo(0).wait_send())
    pl.when(band < NB - 1)(lambda: out_halo(1).wait_send())

    def sent(j, _):
        @pl.when(j != me)
        def _():
            predicted_copy(j, me).wait_send()
            gradient_copy(j, me).wait_send()
        return 0

    lax.fori_loop(0, NM, sent, 0)


def on_device(states, noise_field, target, w_conv, w_proj, matchings):
    numbers = jnp.arange(MEMBERS, dtype=jnp.int32)
    hits = matchings[:, :, None] == numbers[None, None, :]
    inverse = jnp.sum(jnp.where(hits, numbers[None, :, None], 0), axis=1).astype(jnp.int32)
    vmem = pl.BlockSpec(memory_space=pltpu.VMEM)
    smem = pl.BlockSpec(memory_space=pltpu.SMEM)
    D = pltpu.SemaphoreType.DMA
    S = pltpu.VMEM
    scratch = [
        S((2, VP * R, C), F32), S((2, R + 2, KP, C), BF16), S((2, 2, VP, C), BF16), S((2, 2, VP, C), BF16),
        S((H, 3 * KP), BF16), S((KP, 3 * H), BF16), S((VP, H), BF16), S((H, VP), BF16),
        S((2, R, H, C), BF16), S((2, R, H, C), F32), S((4, 2 * VP, 2 * C), BF16),
        S((NM, 2, VP, C), BF16), S((NM, 2, VP, C), BF16), S((MEMBERS, VP, C), F32),
        S((VP * R, C), F32), S((8, VP, C), F32), S(((NK + 1) * MEMBERS * 8, C), F32), S(((NK + 1) * MEMBERS, C), F32),
        S((NM, 2, VP, C), BF16), S((NM, 2, VP, C), BF16), S((2, R, VP, C), BF16),
        S((2, R + 2, H, C), BF16), S((2, VP * R, C), F32),
        S((2, 2, VQ, C), F32), S((2, 2, VQ, C), F32),
        *[S((H, w), F32) for w in CHUNKS],
        *[S((8, 32, w), BF16) for _ in range(4) for w in CHUNKS],
        S((NB, 4, sum(CHUNKS)), F32), S((NB, 4, sum(CHUNKS)), F32),
        D((2,)), D((2,)), D((NM,)), D((NM,)), D((NM,)), D((NM,)), D((2,)), D((2,)),
        D((3,)), D((3,)), D((3, 8)), D((3, 8)), D((NB,)), D((NB,)),
    ]
    grad_states, sums = pl.pallas_call(
        kernel,
        out_shape=(
            jax.ShapeDtypeStruct(states.shape, BF16),
            jax.ShapeDtypeStruct((4, sum(CHUNKS)), F32),
        ),
        in_specs=[vmem] * 7 + [smem] * 2,
        out_specs=(vmem, vmem),
        scratch_shapes=scratch,
        compiler_params=pltpu.CompilerParams(
            collective_id=0, has_side_effects=True, vmem_limit_bytes=60 * 1024 * 1024
        ),
    )(
        states, noise_field, target, w_conv, w_proj,
        jnp.asarray(selection()), jnp.asarray(patch_order()), matchings, inverse,
    )
    parts = []
    for base in (0, 384, 640):
        part = sums[:, base:base + KP]
        for co in range(3):
            parts += [part[:, co * 80:(co + 1) * 80], part[:, 240 + co * 4:244 + co * 4]]
    return grad_states, jnp.concatenate(parts, axis=1), sums[:, KP:KP + V].T


def solution(mesh):
    return jax.shard_map(
        on_device,
        mesh=mesh,
        in_specs=(
            P("member", None, "band", None),
            P("member", None, "band", None),
            P(None, "band", None),
            P(),
            P(),
            P(),
        ),
        out_specs=(
            P("member", None, "band", None),
            P(("member", "band"), None),
            P(None, ("member", "band")),
        ),
        check_vma=False,
    )
```

```python
import functools

import jax
import jax.numpy as jnp
import ml_dtypes
import numpy as np
from jax import lax
from jax.experimental import pallas as pl
from jax.experimental.pallas import tpu as pltpu
from jax.sharding import PartitionSpec as P

F32, BF16 = jnp.float32, jnp.bfloat16
MESH = pl.DeviceIdType.MESH
V, VP, VQ = 84, 96, 88
VH = VP // 2
R, C, H = 16, 128, 512
NM, NB, NK = 16, 8, 4
MEMBERS = 2 * NM
KP = 256
CHUNKS = (384, 256, 256)


def patch_order():
    table = np.zeros((8, 8 * C, C), ml_dtypes.bfloat16)
    for row in range(8):
        for lon in range(C):
            group, patch, col = lon // 8, lon % 8 // 4, lon % 4
            table[group // 2, row * C + lon, group % 2 * 64 + (row * 4 + col) * 2 + patch] = 1
    return table


def remote(src, dst, send_sem, recv_sem, **device):
    return pltpu.make_async_remote_copy(
        src_ref=src, dst_ref=dst, send_sem=send_sem, recv_sem=recv_sem,
        device_id=device, device_id_type=MESH,
    )


def gelu_and_slope(x):
    phi = 0.5 * (1.0 + lax.erf(x * 0.7071067811865476))
    return x * phi, phi + x * (jnp.exp(-0.5 * x * x) * 0.3989422804014327)


def dot(a, b):
    return jnp.dot(a, b, preferred_element_type=F32)


def dot_nt(a, b):
    return lax.dot_general(a, b, (((1,), (1,)), ((), ())), preferred_element_type=F32)


def kernel(
    states_in, noise_in, target_in, w_conv_in, w_proj_in, perm_in, match, match_v,
    out, sums,
    states, noise, target, w_conv, w_proj, perm, inverse_v, inverse, wide_w, load,
    xf, x3, hs, hb, wf, wt, wp, wpt, hidden, slope, pn, sb, rb, pf, tf, tp, es, sc, gb, gr, gn, gp, of,
    hsb, hrb, a0, a1, a2, s10, s11, s12, r10, r11, r12, s20, s21, s22, r20, r21, r22, s3, r3,
    h_send, h_recv, p_send, p_recv, g_send, g_recv, o_send, o_recv,
    u_send, u_recv, v_send, v_recv, w_send, w_recv,
):
    me, band = lax.axis_index("member"), lax.axis_index("band")
    core, chip = lax.rem(me, 2), lax.div(me, 2)
    lanes = lax.broadcasted_iota(jnp.int32, (VP, C), 1)
    acc = (a0, a1, a2)
    s1, r1, s2, r2 = (s10, s11, s12), (r10, r11, r12), (s20, s21, s22), (r20, r21, r22)

    halves = lax.broadcasted_iota(jnp.int32, (VH, C), 1) < 64
    loads = [
        pltpu.make_async_copy(a, b, load.at[k])
        for k, (a, b) in enumerate((
            (noise_in, noise), (states_in, states), (target_in, target),
            (w_conv_in, w_conv), (w_proj_in, w_proj), (perm_in, perm),
        ))
    ]
    for copy in loads:
        copy.start()
    barrier = pltpu.get_barrier_semaphore()

    def greet_member(step, _):
        pl.semaphore_signal(barrier, inc=1, device_id={"member": lax.rem(me + step, NM)}, device_id_type=MESH)
        return 0

    def greet_band(step, _):
        pl.semaphore_signal(barrier, inc=1, device_id={"band": lax.rem(band + step, NB)}, device_id_type=MESH)
        return 0

    lax.fori_loop(1, NM, greet_member, 0)
    lax.fori_loop(1, NB, greet_band, 0)

    to_member = lax.broadcasted_iota(jnp.int32, (MEMBERS, MEMBERS), 0)
    number = lax.broadcasted_iota(jnp.int32, (MEMBERS, MEMBERS), 1)
    column = lax.broadcasted_iota(jnp.int32, (MEMBERS, C), 1)
    table = jnp.zeros((MEMBERS, C), jnp.int32)
    for k in range(NK):
        hit = jnp.where(match_v[k:k + 1, :] == to_member, number, 0)
        table = jnp.where(column == k, jnp.max(hit, axis=1, keepdims=True), table)
    inverse_v[...] = table
    to_scalars = pltpu.make_async_copy(inverse_v, inverse, load.at[6])
    to_scalars.start()

    for copy in loads[:3]:
        copy.wait()
    def add_inputs(c, _):
        part = pl.ds(c * 12, 12)
        to = pl.ds(pl.multiple_of(c * 192, 192), 192)
        for m in range(2):
            value = (states[m, part].astype(F32) + noise[m, part]).astype(BF16).astype(F32)
            xf[m, to, :] = value.reshape(192, C)
        tf[to, :] = target[part].astype(F32).reshape(192, C)
        return 0

    lax.fori_loop(0, V // 12, add_inputs, 0)
    for m in range(2):
        xf[m, V * R:, :] = jnp.zeros(((VP - V) * R, C), F32)
    tf[V * R:, :] = jnp.zeros(((VP - V) * R, C), F32)

    for side, row in ((0, 0), (1, R - 1)):
        for m in range(2):
            hs[side, m] = xf[m, pl.ds(row, VP, stride=R), :].astype(BF16)

    pl.semaphore_wait(barrier, NM + NB - 2)
    def halo(side):
        to = band - 1 if side == 0 else band + 1
        return remote(hs.at[side], hb.at[1 - side], h_send.at[side], h_recv.at[1 - side], band=to)

    pl.when(band > 0)(lambda: halo(0).start())
    pl.when(band < NB - 1)(lambda: halo(1).start())

    def put_row(m, slot, x):
        left = jnp.where(lanes == 0, 0.0, pltpu.roll(x, 1, 1))
        right = jnp.where(lanes == C - 1, 0.0, pltpu.roll(x, C - 1, 1))
        x3[m, slot, 0:80, :] = left[0:80].astype(BF16)
        x3[m, slot, 80:160, :] = x[0:80].astype(BF16)
        x3[m, slot, 160:240, :] = right[0:80].astype(BF16)
        first = left[80:88] + pltpu.roll(x[80:88], 4, 0)
        x3[m, slot, 240:256, :] = jnp.concatenate([first, right[80:88]], axis=0).astype(BF16)

    def build(r, _):
        for m in range(2):
            put_row(m, r + 1, xf[m, pl.ds(r, VP, stride=R), :])
        return 0

    lax.fori_loop(0, R, build, 0)

    for copy in loads[3:]:
        copy.wait()
    wide_w[...] = w_conv[...].astype(F32)
    for ro in range(3):
        base = ro * 3 * V
        parts = [wide_w[base + co * V:base + co * V + 80, :] for co in range(3)]
        parts += [wide_w[base + co * V + 80:base + (co + 1) * V, :] for co in range(3)]
        w_part = jnp.concatenate(parts + [jnp.zeros((KP - 3 * V, H), F32)], axis=0)
        wt[:, ro * H:(ro + 1) * H] = w_part.astype(BF16)
        wf[:, ro * KP:(ro + 1) * KP] = w_part.T.astype(BF16)
    w_pad = jnp.concatenate([w_proj[...].astype(F32), jnp.zeros((VP - V, H), F32)], axis=0)
    wp[...] = w_pad.astype(BF16)
    wpt[...] = w_pad.T.astype(BF16)

    def halo_in(side, slot):
        remote(hs.at[1 - side], hb.at[side], h_send.at[1 - side], h_recv.at[side], band=band).wait_recv()
        for m in range(2):
            put_row(m, slot, hb[side, m].astype(F32))

    def no_halo(slot):
        for m in range(2):
            x3[m, slot] = jnp.zeros((KP, C), BF16)

    pl.when(band > 0)(lambda: halo_in(0, 0))
    pl.when(band == 0)(lambda: no_halo(0))
    pl.when(band < NB - 1)(lambda: halo_in(1, R + 1))
    pl.when(band == NB - 1)(lambda: no_halo(R + 1))
    pl.when(band > 0)(lambda: halo(0).wait_send())
    pl.when(band < NB - 1)(lambda: halo(1).wait_send())

    def pair(ref, m, i):
        return jnp.concatenate([ref[m, i], ref[m, i + 1]], axis=1)

    def order():
        return jnp.concatenate([perm[t] for t in range(8)], axis=1)

    def half_turn(a):
        return pltpu.roll(a, 64, 1)

    def predicted_copy(pr, j, source):
        return remote(sb.at[pr, j], rb.at[pr, source], p_send.at[pr, j], p_recv.at[pr, source], member=j)

    def predict(pr):
        def forward(rp, _):
            i = pr * 8 + rp * 2
            for m in range(2):
                columns = jnp.concatenate([pair(x3, m, i + ro) for ro in range(3)], axis=0)
                pre = dot(wf[...], columns)
                value, grad = gelu_and_slope(pre)
                value = value.astype(BF16)
                for k in range(2):
                    hidden[m, i + k] = value[:, k * C:(k + 1) * C]
                    slope[m, i + k] = grad[:, k * C:(k + 1) * C]
                own = jnp.concatenate([xf[m, pl.ds(i + k, VP, stride=R), :] for k in range(2)], axis=1)
                pn[rp, m * VP:(m + 1) * VP, :] = (own + dot(wp[...], value)).astype(BF16)
            return 0

        lax.fori_loop(0, 4, forward, 0)
        moved = dot(jnp.concatenate([pn[rp] for rp in range(4)], axis=1), order())
        for t in range(8):
            for m in range(2):
                low = moved[m * VP:m * VP + VH, t * C:(t + 1) * C]
                high = moved[m * VP + VH:(m + 1) * VP, t * C:(t + 1) * C]
                sb[pr, 2 * t, m] = jnp.where(halves, low, half_turn(high)).astype(BF16)
                sb[pr, 2 * t + 1, m] = jnp.where(halves, half_turn(low), high).astype(BF16)

        def send(step, _):
            j = lax.rem(me + step, NM)
            predicted_copy(pr, j, me).start()
            return 0

        lax.fori_loop(1, NM, send, 0)
        rb[pr, me] = sb[pr, me]

    def truth_patches():
        rows = [
            jnp.concatenate([tf[pl.ds(pr * 8 + r, VP, stride=R), :] for r in range(8)], axis=1)
            for pr in range(2)
        ]
        moved = dot(jnp.concatenate(rows, axis=0).astype(BF16), perm[chip])
        for pr in range(2):
            low, high = moved[pr * VP:pr * VP + VH], moved[pr * VP + VH:(pr + 1) * VP]
            first = jnp.where(halves, low, half_turn(high))
            second = jnp.where(halves, half_turn(low), high)
            tp[pr] = jnp.where(core == 0, first, second)

    def square(d):
        d = d * d
        total = d[0:8]
        for k in range(1, VH // 8):
            total = total + d[k * 8:(k + 1) * 8]
        return total

    def gradient_copy(pr, j, source):
        return remote(gb.at[pr, j], gr.at[pr, source], g_send.at[pr, j], g_recv.at[pr, source], member=j)

    def score(pr):
        def arrive(step, _):
            source = lax.rem(me + step, NM)
            predicted_copy(pr, source, source).wait_recv()
            return 0

        lax.fori_loop(1, NM, arrive, 0)

        def widen(source, _):
            for m in range(2):
                pf[source * 2 + m] = rb[pr, source, m].astype(F32)
            return 0

        lax.fori_loop(0, NM, widen, 0)

        def edges(m, _):
            own = pf[m]
            es[pl.ds(pl.multiple_of((NK * MEMBERS + m) * 8, 8), 8), :] = square(own - tp[pr])
            for k in range(NK):
                es[pl.ds(pl.multiple_of((k * MEMBERS + m) * 8, 8), 8), :] = square(own - pf[match[k, m]])
            return 0

        lax.fori_loop(0, MEMBERS, edges, 0)
        count = (NK + 1) * MEMBERS
        total = es[pl.ds(0, count, stride=8), :]
        for k in range(1, 8):
            total = total + es[pl.ds(k, count, stride=8), :]
        for shift in (2, 4, 8, 16, 32, 64):
            total = total + pltpu.roll(total, shift, 1)
        sc[...] = lax.rsqrt(total / (32.0 * V) + 1e-06)

        def member_grad(j):
            for mm in range(2):
                m = j * 2 + mm
                own = pf[m]
                pairs = jnp.zeros((VH, C), F32)
                for k in range(NK):
                    n, n_inv = match[k, m], inverse[m, k]
                    pairs = pairs + (own - pf[n]) * sc[pl.ds(k * MEMBERS + m, 1), :]
                    pairs = pairs + (own - pf[n_inv]) * sc[pl.ds(k * MEMBERS + n_inv, 1), :]
                truth = (own - tp[pr]) * sc[pl.ds(NK * MEMBERS + m, 1), :]
                gb[pr, j, mm] = (truth - pairs * (0.5 / NK)).astype(BF16)

        def member_pair(step, _):
            j = lax.rem(me + step, NM)
            member_grad(j)
            gradient_copy(pr, j, me).start()
            return 0

        lax.fori_loop(1, NM, member_pair, 0)
        member_grad(me)
        gr[pr, me] = gb[pr, me]

    def back_to_rows(pr):
        def gradients_in(step, _):
            source = lax.rem(me + step, NM)
            gradient_copy(pr, source, source).wait_recv()
            return 0

        lax.fori_loop(1, NM, gradients_in, 0)
        parts = []
        for t in range(8):
            rows = []
            for m in range(2):
                first, second = gr[pr, 2 * t, m].astype(F32), gr[pr, 2 * t + 1, m].astype(F32)
                rows.append(jnp.where(halves, first, half_turn(second)))
                rows.append(jnp.where(halves, half_turn(first), second))
            parts.append(jnp.concatenate(rows, axis=0).astype(BF16))
        back = dot_nt(jnp.concatenate(parts, axis=1), order()).astype(BF16)
        for m in range(2):
            for r in range(8):
                gn[m, pr * 8 + r] = back[m * VP:(m + 1) * VP, r * C:(r + 1) * C]

        def hidden_grad(rp, _):
            i = pr * 8 + rp * 2
            for m in range(2):
                dh = dot(wpt[...], pair(gn, m, i))
                for k in range(2):
                    gp[m, i + k + 1] = (dh[:, k * C:(k + 1) * C] * slope[m, i + k]).astype(BF16)
            return 0

        lax.fori_loop(0, 4, hidden_grad, 0)

    def wide(ref, i):
        return jnp.concatenate([ref[m, i + k] for m in range(2) for k in range(8)], axis=1)

    def conv_term(ro, pr):
        term = dot_nt(wide(gp, pr * 8 + 1), wide(x3, pr * 8 + ro))
        acc[ro][:, 0:KP] = term if pr == 0 else acc[ro][:, 0:KP] + term

    def proj_term(pr):
        term = dot_nt(wide(hidden, pr * 8), wide(gn, pr * 8))
        acc[0][:, KP:KP + VP] = term if pr == 0 else acc[0][:, KP:KP + VP] + term

    def core_copy(q):
        return remote(s1[q], r1[q], u_send.at[q], u_recv.at[q], member=me + 1 - 2 * core)

    def core_send(q):
        for c in range(NM // 2):
            base = c * 64 + (1 - core) * 32
            s1[q][c] = acc[q][pl.ds(pl.multiple_of(base, 32), 32), :].astype(BF16)
        core_copy(q).start()

    def chip_copy(q, c, source):
        return remote(s2[q].at[c], r2[q].at[source], v_send.at[q, c], v_recv.at[q, source], member=2 * c + core)

    def chip_send(q):
        core_copy(q).wait()
        for c in range(NM // 2):
            base = c * 64 + core * 32
            s2[q][c] = (acc[q][pl.ds(pl.multiple_of(base, 32), 32), :] + r1[q][c].astype(F32)).astype(BF16)

        def send(step, _):
            c = lax.rem(chip + step, NM // 2)
            chip_copy(q, c, chip).start()
            return 0

        lax.fori_loop(1, NM // 2, send, 0)

    def chip_sum(q):
        def take(step, total):
            c = lax.rem(chip + step, NM // 2)
            chip_copy(q, c, c).wait_recv()
            chip_copy(q, c, c).wait_send()
            return total + r2[q][c].astype(F32)

        return lax.fori_loop(1, NM // 2, take, s2[q][chip].astype(F32))

    def band_copy(b, source):
        return remote(s3.at[b], r3.at[source], w_send.at[b], w_recv.at[source], band=b)

    predict(0)
    predict(1)
    truth_patches()
    gp_zero = jnp.zeros((H, C), BF16)
    for m in range(2):
        gp[m, 0] = gp_zero
        gp[m, R + 1] = gp_zero
    acc[0][:, KP:] = jnp.zeros((H, 128), F32)
    to_scalars.wait()
    score(0)
    score(1)
    back_to_rows(0)
    proj_term(0)
    for ro in range(3):
        conv_term(ro, 0)
    back_to_rows(1)
    proj_term(1)
    conv_term(0, 1)
    core_send(0)
    conv_term(1, 1)
    core_send(1)
    chip_send(0)
    conv_term(2, 1)
    core_send(2)
    chip_send(1)

    def fold(d):
        def spread(a):
            return (
                jnp.where(lanes[0:a.shape[0]] == C - 1, 0.0, pltpu.roll(a, C - 1, 1)),
                jnp.where(lanes[0:a.shape[0]] == 0, 0.0, pltpu.roll(a, 1, 1)),
            )
        body = spread(d[0:80])[0] + d[80:160] + spread(d[160:240])[1]
        last = spread(d[240:248])[0] + pltpu.roll(d[240:248], 4, 0) + spread(d[248:256])[1]
        return jnp.concatenate([body, last], axis=0)

    for side, ro, row in ((0, 0, 1), (1, 2, R)):
        rows = jnp.concatenate([gp[0, row], gp[1, row]], axis=1)
        d = dot(wt[:, ro * H:(ro + 1) * H], rows)
        for m in range(2):
            edge = jnp.concatenate([fold(d[:, m * C:(m + 1) * C]), jnp.zeros((VP - VQ, C), F32)], axis=0)
            hsb[side, m] = edge.astype(BF16)

    def out_halo(side):
        to = band - 1 if side == 0 else band + 1
        return remote(hsb.at[side], hrb.at[1 - side], o_send.at[side], o_recv.at[1 - side], band=to)

    pl.when(band > 0)(lambda: out_halo(0).start())
    pl.when(band < NB - 1)(lambda: out_halo(1).start())

    def input_grad(m):
        def step(rp, _):
            i = rp * 2
            rows = jnp.concatenate([pair(gp, m, i + 2 - ro) for ro in range(3)], axis=0)
            d = dot(wt[...], rows)
            for k in range(2):
                value = fold(d[:, k * C:(k + 1) * C]) + gn[m, i + k].astype(F32)[0:VQ]
                of[m, pl.ds(i + k, VQ, stride=R), :] = value
            return 0

        lax.fori_loop(0, R // 2, step, 0)

    chip_send(2)
    input_grad(0)
    for q, width, base in ((0, 384, 0), (1, 256, 384), (2, 256, 640)):
        total = chip_sum(q)
        for b in range(NB):
            s3[b, :, base:base + width] = total[b * 4:(b + 1) * 4]

    def band_send(step, _):
        b = lax.rem(band + step, NB)
        band_copy(b, band).start()
        return 0

    lax.fori_loop(1, NB, band_send, 0)
    input_grad(1)

    def out_halo_in(side, row):
        remote(hsb.at[1 - side], hrb.at[side], o_send.at[1 - side], o_recv.at[side], band=band).wait_recv()
        for m in range(2):
            of[m, pl.ds(row, VQ, stride=R), :] += hrb[side, m].astype(F32)[0:VQ]

    pl.when(band > 0)(lambda: out_halo_in(0, 0))
    pl.when(band < NB - 1)(lambda: out_halo_in(1, R - 1))

    def write(c, _):
        for m in range(2):
            value = of[m, pl.ds(pl.multiple_of(c * 192, 192), 192), :]
            out[m, pl.ds(c * 12, 12)] = value.reshape(12, R, C).astype(BF16)
        return 0

    lax.fori_loop(0, V // 12, write, 0)

    def band_take(step, total):
        b = lax.rem(band + step, NB)
        band_copy(b, b).wait_recv()
        band_copy(b, b).wait_send()
        return total + r3[b]

    total = lax.fori_loop(1, NB, band_take, s3[band])
    sums[...] = total * (1.0 / (MEMBERS * NB * R * C) ** 0.5)

    pl.when(band > 0)(lambda: out_halo(0).wait_send())
    pl.when(band < NB - 1)(lambda: out_halo(1).wait_send())

    def sent(step, _):
        j = lax.rem(me + step, NM)
        for pr in range(2):
            predicted_copy(pr, j, me).wait_send()
            gradient_copy(pr, j, me).wait_send()
        return 0

    lax.fori_loop(1, NM, sent, 0)


def finish(grads, sums, out, conv, proj):
    out[...] = grads[...]
    parts = []
    for base in (0, 384, 640):
        for co in range(3):
            parts += [sums[:, base + co * 80:base + (co + 1) * 80], sums[:, base + 240 + co * 4:base + 244 + co * 4]]
    conv[...] = jnp.concatenate(parts, axis=1)
    proj[...] = sums[:, KP:KP + V]


def on_device(states, noise_field, target, w_conv, w_proj, matchings):
    vmem = pl.BlockSpec(memory_space=pltpu.VMEM)
    smem = pl.BlockSpec(memory_space=pltpu.SMEM)
    D = pltpu.SemaphoreType.DMA
    S = pltpu.VMEM
    hbm = pl.BlockSpec(memory_space=pl.ANY)
    scratch = [
        S(states.shape, BF16), S(noise_field.shape, F32), S(target.shape, BF16), S((9 * V, H), BF16), S((V, H), BF16),
        S((8, 8 * C, C), BF16), S((MEMBERS, C), jnp.int32), pltpu.SMEM((MEMBERS, C), jnp.int32), S((9 * V, H), F32), D((7,)),
        S((2, VP * R, C), F32), S((2, R + 2, KP, C), BF16), S((2, 2, VP, C), BF16), S((2, 2, VP, C), BF16),
        S((H, 3 * KP), BF16), S((KP, 3 * H), BF16), S((VP, H), BF16), S((H, VP), BF16),
        S((2, R, H, C), BF16), S((2, R, H, C), F32), S((4, 2 * VP, 2 * C), BF16),
        S((2, NM, 2, VH, C), BF16), S((2, NM, 2, VH, C), BF16), S((MEMBERS, VH, C), F32),
        S((VP * R, C), F32), S((2, VH, C), F32), S(((NK + 1) * MEMBERS * 8, C), F32), S(((NK + 1) * MEMBERS, C), F32),
        S((2, NM, 2, VH, C), BF16), S((2, NM, 2, VH, C), BF16), S((2, R, VP, C), BF16),
        S((2, R + 2, H, C), BF16), S((2, VP * R, C), F32),
        S((2, 2, VP, C), BF16), S((2, 2, VP, C), BF16),
        *[S((H, w), F32) for w in CHUNKS],
        *[S((8, 32, w), BF16) for _ in range(4) for w in CHUNKS],
        S((NB, 4, sum(CHUNKS)), F32), S((NB, 4, sum(CHUNKS)), F32),
        D((2,)), D((2,)), D((2, NM)), D((2, NM)), D((2, NM)), D((2, NM)), D((2,)), D((2,)),
        D((3,)), D((3,)), D((3, 8)), D((3, 8)), D((NB,)), D((NB,)),
    ]
    grad_states, sums = pl.pallas_call(
        kernel,
        out_shape=(
            jax.ShapeDtypeStruct(states.shape, BF16),
            jax.ShapeDtypeStruct((4, sum(CHUNKS)), F32),
        ),
        in_specs=[hbm] * 6 + [smem, vmem],
        out_specs=(vmem, vmem),
        scratch_shapes=scratch,
        compiler_params=pltpu.CompilerParams(
            collective_id=0, has_side_effects=True, vmem_limit_bytes=60 * 1024 * 1024
        ),
    )(
        states, noise_field, target, w_conv.T, w_proj, jnp.asarray(patch_order()), matchings, matchings,
    )
    grad_states, grad_conv, grad_proj = pl.pallas_call(
        finish,
        out_shape=(
            jax.ShapeDtypeStruct(states.shape, BF16),
            jax.ShapeDtypeStruct((4, 9 * V), F32),
            jax.ShapeDtypeStruct((4, V), F32),
        ),
        in_specs=[vmem] * 2,
        out_specs=(vmem,) * 3,
    )(grad_states, sums)
    return grad_states, grad_conv, grad_proj.T


def solution(mesh):
    return jax.shard_map(
        on_device,
        mesh=mesh,
        in_specs=(
            P("member", None, "band", None),
            P("member", None, "band", None),
            P(None, "band", None),
            P(),
            P(),
            P(),
        ),
        out_specs=(
            P("member", None, "band", None),
            P(("member", "band"), None),
            P(None, ("member", "band")),
        ),
        check_vma=False,
    )
```

```python
import functools

import jax
import jax.numpy as jnp
import ml_dtypes
import numpy as np
from jax import lax
from jax.experimental import pallas as pl
from jax.experimental.pallas import tpu as pltpu
from jax.sharding import PartitionSpec as P

F32, BF16 = jnp.float32, jnp.bfloat16
MESH = pl.DeviceIdType.MESH
V, VP, VQ = 84, 96, 88
VH = VP // 2
R, C, H = 16, 128, 512
NM, NB, NK = 16, 8, 4
MEMBERS = 2 * NM
KP = 256
CHUNKS = (384, 256, 256)


def patch_order():
    table = np.zeros((8, 8 * C, C), ml_dtypes.bfloat16)
    for row in range(8):
        for lon in range(C):
            group, patch, col = lon // 8, lon % 8 // 4, lon % 4
            table[group // 2, row * C + lon, group % 2 * 64 + (row * 4 + col) * 2 + patch] = 1
    return table


def remote(src, dst, send_sem, recv_sem, **device):
    return pltpu.make_async_remote_copy(
        src_ref=src, dst_ref=dst, send_sem=send_sem, recv_sem=recv_sem,
        device_id=device, device_id_type=MESH,
    )


def gelu_and_slope(x):
    phi = 0.5 + 0.5 * lax.erf(x * 0.7071067811865476)
    bell = jnp.exp2((x * x) * (-0.5 * 1.4426950408889634) - 1.3257480647361593)
    return x * phi, phi + x * bell


def dot(a, b):
    return jnp.dot(a, b, preferred_element_type=F32)


def dot_nt(a, b):
    return lax.dot_general(a, b, (((1,), (1,)), ((), ())), preferred_element_type=F32)


def kernel(
    states_in, noise_in, target_in, w_conv_in, w_proj_in, perm_in, match, match_v,
    out, sums,
    states, noise, target, w_conv, w_proj, perm, inverse_v, inverse, wide_w, load,
    xf, x3, hs, hb, wf, wt, wp, wpt, hidden, slope, pn, sb, rb, pf, tf, tp, es, sc, gb, gr, gn, gp, of,
    hsb, hrb, a0, a1, a2, s10, s11, s12, r10, r11, r12, s20, s21, s22, r20, r21, r22, s3, r3,
    h_send, h_recv, p_send, p_recv, g_send, g_recv, o_send, o_recv,
    u_send, u_recv, v_send, v_recv, w_send, w_recv,
):
    me, band = lax.axis_index("member"), lax.axis_index("band")
    core, chip = lax.rem(me, 2), lax.div(me, 2)
    lanes = lax.broadcasted_iota(jnp.int32, (VP, C), 1)
    acc = (a0, a1, a2)
    s1, r1, s2, r2 = (s10, s11, s12), (r10, r11, r12), (s20, s21, s22), (r20, r21, r22)

    halves = lax.broadcasted_iota(jnp.int32, (VH, C), 1) < 64
    loads = [
        pltpu.make_async_copy(a, b, load.at[k])
        for k, (a, b) in enumerate((
            (w_conv_in, w_conv), (w_proj_in, w_proj), (noise_in, noise), (states_in, states),
            (target_in, target), (perm_in, perm),
        ))
    ]
    for copy in loads:
        copy.start()
    barrier = pltpu.get_barrier_semaphore()

    def greet_member(step, _):
        pl.semaphore_signal(barrier, inc=1, device_id={"member": lax.rem(me + step, NM)}, device_id_type=MESH)
        return 0

    def greet_band(step, _):
        pl.semaphore_signal(barrier, inc=1, device_id={"band": lax.rem(band + step, NB)}, device_id_type=MESH)
        return 0

    lax.fori_loop(1, NM, greet_member, 0)
    lax.fori_loop(1, NB, greet_band, 0)

    to_member = lax.broadcasted_iota(jnp.int32, (MEMBERS, MEMBERS), 0)
    number = lax.broadcasted_iota(jnp.int32, (MEMBERS, MEMBERS), 1)
    column = lax.broadcasted_iota(jnp.int32, (MEMBERS, C), 1)
    table = jnp.zeros((MEMBERS, C), jnp.int32)
    for k in range(NK):
        hit = jnp.where(match_v[k:k + 1, :] == to_member, number, 0)
        table = jnp.where(column == k, jnp.max(hit, axis=1, keepdims=True), table)
    inverse_v[...] = table
    to_scalars = pltpu.make_async_copy(inverse_v, inverse, load.at[6])
    to_scalars.start()

    for copy in loads[:2]:
        copy.wait()
    wide_w[...] = w_conv[...].astype(F32)
    for ro in range(3):
        base = ro * 3 * V
        parts = [wide_w[base + co * V:base + co * V + 80, :] for co in range(3)]
        parts += [wide_w[base + co * V + 80:base + (co + 1) * V, :] for co in range(3)]
        w_part = jnp.concatenate(parts + [jnp.zeros((KP - 3 * V, H), F32)], axis=0)
        wt[:, ro * H:(ro + 1) * H] = w_part.astype(BF16)
        wf[:, ro * KP:(ro + 1) * KP] = w_part.T.astype(BF16)
    w_pad = jnp.concatenate([w_proj[...].astype(F32), jnp.zeros((VP - V, H), F32)], axis=0)
    wp[...] = w_pad.astype(BF16)
    wpt[...] = w_pad.T.astype(BF16)

    for copy in loads[2:5]:
        copy.wait()
    def add_inputs(c, _):
        part = pl.ds(c * 12, 12)
        to = pl.ds(pl.multiple_of(c * 192, 192), 192)
        for m in range(2):
            value = (states[m, part].astype(F32) + noise[m, part]).astype(BF16).astype(F32)
            xf[m, to, :] = value.reshape(192, C)
        tf[to, :] = target[part].astype(F32).reshape(192, C)
        return 0

    lax.fori_loop(0, V // 12, add_inputs, 0)
    for m in range(2):
        xf[m, V * R:, :] = jnp.zeros(((VP - V) * R, C), F32)
    tf[V * R:, :] = jnp.zeros(((VP - V) * R, C), F32)

    for side, row in ((0, 0), (1, R - 1)):
        for m in range(2):
            hs[side, m] = xf[m, pl.ds(row, VP, stride=R), :].astype(BF16)

    def put_row(m, slot, x):
        left = jnp.where(lanes == 0, 0.0, pltpu.roll(x, 1, 1))
        right = jnp.where(lanes == C - 1, 0.0, pltpu.roll(x, C - 1, 1))
        x3[m, slot, 0:80, :] = left[0:80].astype(BF16)
        x3[m, slot, 80:160, :] = x[0:80].astype(BF16)
        x3[m, slot, 160:240, :] = right[0:80].astype(BF16)
        first = left[80:88] + pltpu.roll(x[80:88], 4, 0)
        x3[m, slot, 240:256, :] = jnp.concatenate([first, right[80:88]], axis=0).astype(BF16)

    def build(r, _):
        for m in range(2):
            put_row(m, r + 1, xf[m, pl.ds(r, VP, stride=R), :])
        return 0

    lax.fori_loop(0, R, build, 0)

    loads[5].wait()
    pl.semaphore_wait(barrier, NM + NB - 2)
    def halo(side):
        to = band - 1 if side == 0 else band + 1
        return remote(hs.at[side], hb.at[1 - side], h_send.at[side], h_recv.at[1 - side], band=to)

    pl.when(band > 0)(lambda: halo(0).start())
    pl.when(band < NB - 1)(lambda: halo(1).start())

    def halo_in(side, slot):
        remote(hs.at[1 - side], hb.at[side], h_send.at[1 - side], h_recv.at[side], band=band).wait_recv()
        for m in range(2):
            put_row(m, slot, hb[side, m].astype(F32))

    def no_halo(slot):
        for m in range(2):
            x3[m, slot] = jnp.zeros((KP, C), BF16)

    def halo_rows():
        pl.when(band > 0)(lambda: halo_in(0, 0))
        pl.when(band == 0)(lambda: no_halo(0))
        pl.when(band < NB - 1)(lambda: halo_in(1, R + 1))
        pl.when(band == NB - 1)(lambda: no_halo(R + 1))

    def pair(ref, m, i):
        return jnp.concatenate([ref[m, i], ref[m, i + 1]], axis=1)

    def order():
        return jnp.concatenate([perm[t] for t in range(8)], axis=1)

    def half_turn(a):
        return pltpu.roll(a, 64, 1)

    def predicted_copy(pr, j, source):
        return remote(sb.at[pr, j], rb.at[pr, source], p_send.at[pr, j], p_recv.at[pr, source], member=j)

    def forward(rp, _):
        i = rp * 2
        for m in range(2):
            columns = jnp.concatenate([pair(x3, m, i + ro) for ro in range(3)], axis=0)
            for part in range(0, H, H // 2):
                rows = slice(part, part + H // 2)
                value, grad = gelu_and_slope(dot(wf[rows, :], columns))
                value = value.astype(BF16)
                for k in range(2):
                    hidden[m, i + k, rows, :] = value[:, k * C:(k + 1) * C]
                    slope[m, i + k, rows, :] = grad[:, k * C:(k + 1) * C]
        return 0

    def predict(pr):
        for m in range(2):
            for r in range(0, 8, 4):
                i = pr * 8 + r
                more = dot(wp[...], jnp.concatenate([hidden[m, i + k] for k in range(4)], axis=1))
                for k in range(0, 4, 2):
                    own = jnp.concatenate([xf[m, pl.ds(i + k + n, VP, stride=R), :] for n in range(2)], axis=1)
                    pn[(r + k) // 2, m * VP:(m + 1) * VP, :] = (own + more[:, k * C:(k + 2) * C]).astype(BF16)
        moved = dot(jnp.concatenate([pn[rp] for rp in range(4)], axis=1), order())
        for t in range(8):
            for m in range(2):
                low = moved[m * VP:m * VP + VH, t * C:(t + 1) * C]
                high = moved[m * VP + VH:(m + 1) * VP, t * C:(t + 1) * C]
                sb[pr, 2 * t, m] = jnp.where(halves, low, half_turn(high)).astype(BF16)
                sb[pr, 2 * t + 1, m] = jnp.where(halves, half_turn(low), high).astype(BF16)

        def send(step, _):
            j = lax.rem(me + step, NM)
            predicted_copy(pr, j, me).start()
            return 0

        lax.fori_loop(1, NM, send, 0)
        rb[pr, me] = sb[pr, me]

    def truth_patches():
        rows = [
            jnp.concatenate([tf[pl.ds(pr * 8 + r, VP, stride=R), :] for r in range(8)], axis=1)
            for pr in range(2)
        ]
        moved = dot(jnp.concatenate(rows, axis=0).astype(BF16), perm[chip])
        for pr in range(2):
            low, high = moved[pr * VP:pr * VP + VH], moved[pr * VP + VH:(pr + 1) * VP]
            first = jnp.where(halves, low, half_turn(high))
            second = jnp.where(halves, half_turn(low), high)
            tp[pr] = jnp.where(core == 0, first, second)

    def square(d):
        d = d * d
        total = d[0:8]
        for k in range(1, VH // 8):
            total = total + d[k * 8:(k + 1) * 8]
        return total

    def gradient_copy(pr, j, source):
        return remote(gb.at[pr, j], gr.at[pr, source], g_send.at[pr, j], g_recv.at[pr, source], member=j)

    def score(pr):
        def arrive(step, _):
            source = lax.rem(me + step, NM)
            predicted_copy(pr, source, source).wait_recv()
            return 0

        lax.fori_loop(1, NM, arrive, 0)

        def widen(source, _):
            for m in range(2):
                pf[source * 2 + m] = rb[pr, source, m].astype(F32)
            return 0

        lax.fori_loop(0, NM, widen, 0)

        def edges(m, _):
            own = pf[m]
            es[pl.ds(pl.multiple_of((NK * MEMBERS + m) * 8, 8), 8), :] = square(own - tp[pr])
            for k in range(NK):
                es[pl.ds(pl.multiple_of((k * MEMBERS + m) * 8, 8), 8), :] = square(own - pf[match[k, m]])
            return 0

        lax.fori_loop(0, MEMBERS, edges, 0)
        count = (NK + 1) * MEMBERS
        total = es[pl.ds(0, count, stride=8), :]
        for k in range(1, 8):
            total = total + es[pl.ds(k, count, stride=8), :]
        for shift in (2, 4, 8, 16, 32, 64):
            total = total + pltpu.roll(total, shift, 1)
        sc[...] = lax.rsqrt(total / (32.0 * V) + 1e-06)

        def member_grad(j):
            for mm in range(2):
                m = j * 2 + mm
                own = pf[m]
                pairs = jnp.zeros((VH, C), F32)
                for k in range(NK):
                    n, n_inv = match[k, m], inverse[m, k]
                    pairs = pairs + (own - pf[n]) * sc[pl.ds(k * MEMBERS + m, 1), :]
                    pairs = pairs + (own - pf[n_inv]) * sc[pl.ds(k * MEMBERS + n_inv, 1), :]
                truth = (own - tp[pr]) * sc[pl.ds(NK * MEMBERS + m, 1), :]
                gb[pr, j, mm] = (truth - pairs * (0.5 / NK)).astype(BF16)

        def member_pair(step, _):
            j = lax.rem(me + step, NM)
            member_grad(j)
            gradient_copy(pr, j, me).start()
            return 0

        lax.fori_loop(1, NM, member_pair, 0)
        member_grad(me)
        gr[pr, me] = gb[pr, me]

    def back_to_rows(pr):
        def gradients_in(step, _):
            source = lax.rem(me + step, NM)
            gradient_copy(pr, source, source).wait_recv()
            return 0

        lax.fori_loop(1, NM, gradients_in, 0)
        parts = []
        for t in range(8):
            rows = []
            for m in range(2):
                first, second = gr[pr, 2 * t, m].astype(F32), gr[pr, 2 * t + 1, m].astype(F32)
                rows.append(jnp.where(halves, first, half_turn(second)))
                rows.append(jnp.where(halves, half_turn(first), second))
            parts.append(jnp.concatenate(rows, axis=0).astype(BF16))
        back = dot_nt(jnp.concatenate(parts, axis=1), order()).astype(BF16)
        for m in range(2):
            for r in range(8):
                gn[m, pr * 8 + r] = back[m * VP:(m + 1) * VP, r * C:(r + 1) * C]

        def hidden_grad(rp, _):
            i = pr * 8 + rp * 2
            for m in range(2):
                dh = dot(wpt[...], pair(gn, m, i))
                for k in range(2):
                    gp[m, i + k + 1] = (dh[:, k * C:(k + 1) * C] * slope[m, i + k]).astype(BF16)
            return 0

        lax.fori_loop(0, 4, hidden_grad, 0)

    def wide(ref, i):
        return jnp.concatenate([ref[m, i + k] for m in range(2) for k in range(8)], axis=1)

    def conv_term(ro, pr):
        term = dot_nt(wide(gp, pr * 8 + 1), wide(x3, pr * 8 + ro))
        acc[ro][:, 0:KP] = term if pr == 0 else acc[ro][:, 0:KP] + term

    def proj_term(pr):
        term = dot_nt(wide(hidden, pr * 8), wide(gn, pr * 8))
        acc[0][:, KP:KP + VP] = term if pr == 0 else acc[0][:, KP:KP + VP] + term

    def core_copy(q):
        return remote(s1[q], r1[q], u_send.at[q], u_recv.at[q], member=me + 1 - 2 * core)

    def core_send(q):
        for c in range(NM // 2):
            base = c * 64 + (1 - core) * 32
            s1[q][c] = acc[q][pl.ds(pl.multiple_of(base, 32), 32), :].astype(BF16)
        core_copy(q).start()

    def chip_copy(q, c, source):
        return remote(s2[q].at[c], r2[q].at[source], v_send.at[q, c], v_recv.at[q, source], member=2 * c + core)

    def chip_send(q):
        core_copy(q).wait_recv()
        for c in range(NM // 2):
            base = c * 64 + core * 32
            s2[q][c] = (acc[q][pl.ds(pl.multiple_of(base, 32), 32), :] + r1[q][c].astype(F32)).astype(BF16)

        def send(step, _):
            c = lax.rem(chip + step, NM // 2)
            chip_copy(q, c, chip).start()
            return 0

        lax.fori_loop(1, NM // 2, send, 0)

    def chip_sum(q):
        def take(step, total):
            c = lax.rem(chip + step, NM // 2)
            chip_copy(q, c, c).wait_recv()
            return total + r2[q][c].astype(F32)

        return lax.fori_loop(1, NM // 2, take, s2[q][chip].astype(F32))

    def band_copy(b, source):
        return remote(s3.at[b], r3.at[source], w_send.at[b], w_recv.at[source], band=b)

    lax.fori_loop(1, 4, forward, 0)
    truth_patches()
    gp_zero = jnp.zeros((H, C), BF16)
    for m in range(2):
        gp[m, 0] = gp_zero
        gp[m, R + 1] = gp_zero
    acc[0][:, KP:] = jnp.zeros((H, 128), F32)
    halo_rows()
    forward(0, 0)
    predict(0)
    lax.fori_loop(4, 8, forward, 0)
    predict(1)
    to_scalars.wait()
    score(0)
    score(1)
    back_to_rows(0)
    proj_term(0)
    for ro in range(3):
        conv_term(ro, 0)
    back_to_rows(1)
    proj_term(1)
    conv_term(0, 1)
    core_send(0)
    conv_term(1, 1)
    core_send(1)
    conv_term(2, 1)
    core_send(2)
    chip_send(0)
    chip_send(1)

    def fold(d):
        def spread(a):
            return (
                jnp.where(lanes[0:a.shape[0]] == C - 1, 0.0, pltpu.roll(a, C - 1, 1)),
                jnp.where(lanes[0:a.shape[0]] == 0, 0.0, pltpu.roll(a, 1, 1)),
            )
        body = spread(d[0:80])[0] + d[80:160] + spread(d[160:240])[1]
        last = spread(d[240:248])[0] + pltpu.roll(d[240:248], 4, 0) + spread(d[248:256])[1]
        return jnp.concatenate([body, last], axis=0)

    for side, ro, row in ((0, 0, 1), (1, 2, R)):
        rows = jnp.concatenate([gp[0, row], gp[1, row]], axis=1)
        d = dot(wt[:, ro * H:(ro + 1) * H], rows)
        for m in range(2):
            edge = jnp.concatenate([fold(d[:, m * C:(m + 1) * C]), jnp.zeros((VP - VQ, C), F32)], axis=0)
            hsb[side, m] = edge.astype(BF16)

    def out_halo(side):
        to = band - 1 if side == 0 else band + 1
        return remote(hsb.at[side], hrb.at[1 - side], o_send.at[side], o_recv.at[1 - side], band=to)

    pl.when(band > 0)(lambda: out_halo(0).start())
    pl.when(band < NB - 1)(lambda: out_halo(1).start())

    def input_grad(m, low, high):
        def step(rp, _):
            i = rp * 2
            rows = jnp.concatenate([pair(gp, m, i + 2 - ro) for ro in range(3)], axis=0)
            d = dot(wt[...], rows)
            for k in range(2):
                value = fold(d[:, k * C:(k + 1) * C]) + gn[m, i + k].astype(F32)[0:VQ]
                of[m, pl.ds(i + k, VQ, stride=R), :] = value
            return 0

        lax.fori_loop(low, high, step, 0)

    chip_send(2)
    input_grad(0, 0, 8)
    input_grad(1, 0, 6)
    for q, width, base in ((0, 384, 0), (1, 256, 384), (2, 256, 640)):
        total = chip_sum(q)
        for b in range(NB):
            s3[b, :, base:base + width] = total[b * 4:(b + 1) * 4]

    def band_send(step, _):
        b = lax.rem(band + step, NB)
        band_copy(b, band).start()
        return 0

    lax.fori_loop(1, NB, band_send, 0)
    input_grad(1, 6, 8)

    def out_halo_in(side, row):
        remote(hsb.at[1 - side], hrb.at[side], o_send.at[1 - side], o_recv.at[side], band=band).wait_recv()
        for m in range(2):
            of[m, pl.ds(row, VQ, stride=R), :] += hrb[side, m].astype(F32)[0:VQ]

    pl.when(band > 0)(lambda: out_halo_in(0, 0))
    pl.when(band < NB - 1)(lambda: out_halo_in(1, R - 1))

    def write(c, _):
        for m in range(2):
            value = of[m, pl.ds(pl.multiple_of(c * 192, 192), 192), :]
            out[m, pl.ds(c * 12, 12)] = value.reshape(12, R, C).astype(BF16)
        return 0

    lax.fori_loop(0, V // 12, write, 0)

    def band_take(step, total):
        b = lax.rem(band + step, NB)
        band_copy(b, b).wait_recv()
        return total + r3[b]

    total = lax.fori_loop(1, NB, band_take, s3[band])
    sums[...] = total * (1.0 / (MEMBERS * NB * R * C) ** 0.5)

    pl.when(band > 0)(lambda: halo(0).wait_send())
    pl.when(band < NB - 1)(lambda: halo(1).wait_send())
    for q in range(3):
        core_copy(q).wait_send()

    def sums_sent(step, _):
        c = lax.rem(chip + step, NM // 2)
        for q in range(3):
            chip_copy(q, c, chip).wait_send()
        band_copy(lax.rem(band + step, NB), band).wait_send()
        return 0

    lax.fori_loop(1, NB, sums_sent, 0)
    pl.when(band > 0)(lambda: out_halo(0).wait_send())
    pl.when(band < NB - 1)(lambda: out_halo(1).wait_send())

    def sent(step, _):
        j = lax.rem(me + step, NM)
        for pr in range(2):
            predicted_copy(pr, j, me).wait_send()
            gradient_copy(pr, j, me).wait_send()
        return 0

    lax.fori_loop(1, NM, sent, 0)


def finish(grads, sums, out, conv, proj):
    out[...] = grads[...]
    parts = []
    for base in (0, 384, 640):
        for co in range(3):
            parts += [sums[:, base + co * 80:base + (co + 1) * 80], sums[:, base + 240 + co * 4:base + 244 + co * 4]]
    conv[...] = jnp.concatenate(parts, axis=1)
    proj[...] = sums[:, KP:KP + V]


def on_device(states, noise_field, target, w_conv, w_proj, matchings):
    vmem = pl.BlockSpec(memory_space=pltpu.VMEM)
    smem = pl.BlockSpec(memory_space=pltpu.SMEM)
    D = pltpu.SemaphoreType.DMA
    S = pltpu.VMEM
    hbm = pl.BlockSpec(memory_space=pl.ANY)
    scratch = [
        S(states.shape, BF16), S(noise_field.shape, F32), S(target.shape, BF16), S((9 * V, H), BF16), S((V, H), BF16),
        S((8, 8 * C, C), BF16), S((MEMBERS, C), jnp.int32), pltpu.SMEM((MEMBERS, C), jnp.int32), S((9 * V, H), F32), D((7,)),
        S((2, VP * R, C), F32), S((2, R + 2, KP, C), BF16), S((2, 2, VP, C), BF16), S((2, 2, VP, C), BF16),
        S((H, 3 * KP), BF16), S((KP, 3 * H), BF16), S((VP, H), BF16), S((H, VP), BF16),
        S((2, R, H, C), BF16), S((2, R, H, C), F32), S((4, 2 * VP, 2 * C), BF16),
        S((2, NM, 2, VH, C), BF16), S((2, NM, 2, VH, C), BF16), S((MEMBERS, VH, C), F32),
        S((VP * R, C), F32), S((2, VH, C), F32), S(((NK + 1) * MEMBERS * 8, C), F32), S(((NK + 1) * MEMBERS, C), F32),
        S((2, NM, 2, VH, C), BF16), S((2, NM, 2, VH, C), BF16), S((2, R, VP, C), BF16),
        S((2, R + 2, H, C), BF16), S((2, VP * R, C), F32),
        S((2, 2, VP, C), BF16), S((2, 2, VP, C), BF16),
        *[S((H, w), F32) for w in CHUNKS],
        *[S((8, 32, w), BF16) for _ in range(4) for w in CHUNKS],
        S((NB, 4, sum(CHUNKS)), F32), S((NB, 4, sum(CHUNKS)), F32),
        D((2,)), D((2,)), D((2, NM)), D((2, NM)), D((2, NM)), D((2, NM)), D((2,)), D((2,)),
        D((3,)), D((3,)), D((3, 8)), D((3, 8)), D((NB,)), D((NB,)),
    ]
    grad_states, sums = pl.pallas_call(
        kernel,
        out_shape=(
            jax.ShapeDtypeStruct(states.shape, BF16),
            jax.ShapeDtypeStruct((4, sum(CHUNKS)), F32),
        ),
        in_specs=[hbm] * 6 + [smem, vmem],
        out_specs=(vmem, vmem),
        scratch_shapes=scratch,
        compiler_params=pltpu.CompilerParams(
            collective_id=0, has_side_effects=True, vmem_limit_bytes=60 * 1024 * 1024
        ),
    )(
        states, noise_field, target, w_conv.T, w_proj, jnp.asarray(patch_order()), matchings, matchings,
    )
    grad_states, grad_conv, grad_proj = pl.pallas_call(
        finish,
        out_shape=(
            jax.ShapeDtypeStruct(states.shape, BF16),
            jax.ShapeDtypeStruct((4, 9 * V), F32),
            jax.ShapeDtypeStruct((4, V), F32),
        ),
        in_specs=[vmem] * 2,
        out_specs=(vmem,) * 3,
    )(grad_states, sums)
    return grad_states, grad_conv, grad_proj.T


def solution(mesh):
    return jax.shard_map(
        on_device,
        mesh=mesh,
        in_specs=(
            P("member", None, "band", None),
            P("member", None, "band", None),
            P(None, "band", None),
            P(),
            P(),
            P(),
        ),
        out_specs=(
            P("member", None, "band", None),
            P(("member", "band"), None),
            P(None, ("member", "band")),
        ),
        check_vma=False,
    )
```

```python
import functools

import jax
import jax.numpy as jnp
import ml_dtypes
import numpy as np
from jax import lax
from jax.experimental import pallas as pl
from jax.experimental.pallas import tpu as pltpu
from jax.sharding import PartitionSpec as P

F32, BF16 = jnp.float32, jnp.bfloat16
MESH = pl.DeviceIdType.MESH
V, VP, VQ = 84, 96, 88
VH = VP // 2
R, C, H = 16, 128, 512
NM, NB, NK = 16, 8, 4
GROUP = NM // 2 * NB
MEMBERS = 2 * NM
KP = 256
CHUNKS = (384, 256, 256)


def patch_order():
    table = np.zeros((8, 8 * C, C), ml_dtypes.bfloat16)
    for row in range(8):
        for lon in range(C):
            group, patch, col = lon // 8, lon % 8 // 4, lon % 4
            table[group // 2, row * C + lon, group % 2 * 64 + (row * 4 + col) * 2 + patch] = 1
    return table


def remote(src, dst, send_sem, recv_sem, **device):
    return pltpu.make_async_remote_copy(
        src_ref=src, dst_ref=dst, send_sem=send_sem, recv_sem=recv_sem,
        device_id=device, device_id_type=MESH,
    )


def gelu_and_slope(x):
    phi = 0.5 + 0.5 * lax.erf(x * 0.7071067811865476)
    bell = jnp.exp2((x * x) * (-0.5 * 1.4426950408889634) - 1.3257480647361593)
    return x * phi, phi + x * bell


def dot(a, b):
    return jnp.dot(a, b, preferred_element_type=F32)


def dot_nt(a, b):
    return lax.dot_general(a, b, (((1,), (1,)), ((), ())), preferred_element_type=F32)


def kernel(
    states_in, noise_in, target_in, w_conv_in, w_proj_in, perm_in, match, match_v,
    out, sums,
    states, noise, target, w_conv, w_proj, perm, inverse_v, inverse, wide_w, load,
    xf, x3, hs, hb, wf, wt, wp, wpt, hidden, slope, pn, sb, rb, pf, tf, tp, es, sc, gb, gr, gn, gp, of,
    hsb, hrb, a0, a1, a2, s10, s11, s12, r10, r11, r12, s3, r3,
    h_send, h_recv, p_send, p_recv, g_send, g_recv, o_send, o_recv,
    u_send, u_recv, w_send, w_recv, ready,
):
    me, band = lax.axis_index("member"), lax.axis_index("band")
    core, chip = lax.rem(me, 2), lax.div(me, 2)
    lanes = lax.broadcasted_iota(jnp.int32, (VP, C), 1)
    acc = (a0, a1, a2)
    s1, r1 = (s10, s11, s12), (r10, r11, r12)
    spot = chip * NB + band

    halves = lax.broadcasted_iota(jnp.int32, (VH, C), 1) < 64
    loads = [
        pltpu.make_async_copy(a, b, load.at[k])
        for k, (a, b) in enumerate((
            (w_conv_in, w_conv), (w_proj_in, w_proj), (noise_in, noise), (states_in, states),
            (target_in, target), (perm_in, perm),
        ))
    ]
    for copy in loads:
        copy.start()
    barrier = pltpu.get_barrier_semaphore()

    def greet_member(step, _):
        pl.semaphore_signal(barrier, inc=1, device_id={"member": lax.rem(me + step, NM)}, device_id_type=MESH)
        return 0

    def greet_band(step, _):
        pl.semaphore_signal(barrier, inc=1, device_id={"band": lax.rem(band + step, NB)}, device_id_type=MESH)
        return 0

    lax.fori_loop(1, NM, greet_member, 0)
    lax.fori_loop(1, NB, greet_band, 0)

    to_member = lax.broadcasted_iota(jnp.int32, (MEMBERS, MEMBERS), 0)
    number = lax.broadcasted_iota(jnp.int32, (MEMBERS, MEMBERS), 1)
    column = lax.broadcasted_iota(jnp.int32, (MEMBERS, C), 1)
    table = jnp.zeros((MEMBERS, C), jnp.int32)
    for k in range(NK):
        hit = jnp.where(match_v[k:k + 1, :] == to_member, number, 0)
        table = jnp.where(column == k, jnp.max(hit, axis=1, keepdims=True), table)
    inverse_v[...] = table
    to_scalars = pltpu.make_async_copy(inverse_v, inverse, load.at[6])
    to_scalars.start()

    for copy in loads[:2]:
        copy.wait()
    wide_w[...] = w_conv[...].astype(F32)
    for ro in range(3):
        base = ro * 3 * V
        parts = [wide_w[base + co * V:base + co * V + 80, :] for co in range(3)]
        parts += [wide_w[base + co * V + 80:base + (co + 1) * V, :] for co in range(3)]
        w_part = jnp.concatenate(parts + [jnp.zeros((KP - 3 * V, H), F32)], axis=0)
        wt[:, ro * H:(ro + 1) * H] = w_part.astype(BF16)
        wf[:, ro * KP:(ro + 1) * KP] = w_part.T.astype(BF16)
    w_pad = jnp.concatenate([w_proj[...].astype(F32), jnp.zeros((VP - V, H), F32)], axis=0)
    wp[...] = w_pad.astype(BF16)
    wpt[...] = w_pad.T.astype(BF16)

    for copy in loads[2:5]:
        copy.wait()
    def add_inputs(c, _):
        part = pl.ds(c * 12, 12)
        to = pl.ds(pl.multiple_of(c * 192, 192), 192)
        for m in range(2):
            value = (states[m, part].astype(F32) + noise[m, part]).astype(BF16).astype(F32)
            xf[m, to, :] = value.reshape(192, C)
        tf[to, :] = target[part].astype(F32).reshape(192, C)
        return 0

    lax.fori_loop(0, V // 12, add_inputs, 0)
    for m in range(2):
        xf[m, V * R:, :] = jnp.zeros(((VP - V) * R, C), F32)
    tf[V * R:, :] = jnp.zeros(((VP - V) * R, C), F32)

    for side, row in ((0, 0), (1, R - 1)):
        for m in range(2):
            hs[side, m] = xf[m, pl.ds(row, VP, stride=R), :].astype(BF16)

    def put_row(m, slot, x):
        left = jnp.where(lanes == 0, 0.0, pltpu.roll(x, 1, 1))
        right = jnp.where(lanes == C - 1, 0.0, pltpu.roll(x, C - 1, 1))
        x3[m, slot, 0:80, :] = left[0:80].astype(BF16)
        x3[m, slot, 80:160, :] = x[0:80].astype(BF16)
        x3[m, slot, 160:240, :] = right[0:80].astype(BF16)
        first = left[80:88] + pltpu.roll(x[80:88], 4, 0)
        x3[m, slot, 240:256, :] = jnp.concatenate([first, right[80:88]], axis=0).astype(BF16)

    def build(r, _):
        for m in range(2):
            put_row(m, r + 1, xf[m, pl.ds(r, VP, stride=R), :])
        return 0

    lax.fori_loop(0, R, build, 0)

    loads[5].wait()
    pl.semaphore_wait(barrier, NM + NB - 2)

    def all_here(step, _):
        pl.semaphore_signal(ready, inc=1, device_id={"band": lax.rem(band + step, NB)}, device_id_type=MESH)
        return 0

    lax.fori_loop(1, NB, all_here, 0)
    def halo(side):
        to = band - 1 if side == 0 else band + 1
        return remote(hs.at[side], hb.at[1 - side], h_send.at[side], h_recv.at[1 - side], band=to)

    pl.when(band > 0)(lambda: halo(0).start())
    pl.when(band < NB - 1)(lambda: halo(1).start())

    def halo_in(side, slot):
        remote(hs.at[1 - side], hb.at[side], h_send.at[1 - side], h_recv.at[side], band=band).wait_recv()
        for m in range(2):
            put_row(m, slot, hb[side, m].astype(F32))

    def no_halo(slot):
        for m in range(2):
            x3[m, slot] = jnp.zeros((KP, C), BF16)

    def halo_rows():
        pl.when(band > 0)(lambda: halo_in(0, 0))
        pl.when(band == 0)(lambda: no_halo(0))
        pl.when(band < NB - 1)(lambda: halo_in(1, R + 1))
        pl.when(band == NB - 1)(lambda: no_halo(R + 1))

    def pair(ref, m, i):
        return jnp.concatenate([ref[m, i], ref[m, i + 1]], axis=1)

    def order():
        return jnp.concatenate([perm[t] for t in range(8)], axis=1)

    def half_turn(a):
        return pltpu.roll(a, 64, 1)

    def predicted_copy(pr, j, source):
        return remote(sb.at[pr, j], rb.at[pr, source], p_send.at[pr, j], p_recv.at[pr, source], member=j)

    def forward(rp, _):
        i = rp * 2
        for m in range(2):
            columns = jnp.concatenate([pair(x3, m, i + ro) for ro in range(3)], axis=0)
            for part in range(0, H, H // 2):
                rows = slice(part, part + H // 2)
                value, grad = gelu_and_slope(dot(wf[rows, :], columns))
                value = value.astype(BF16)
                for k in range(2):
                    hidden[m, i + k, rows, :] = value[:, k * C:(k + 1) * C]
                    slope[m, i + k, rows, :] = grad[:, k * C:(k + 1) * C]
        return 0

    def predict(pr):
        for m in range(2):
            for r in range(0, 8, 4):
                i = pr * 8 + r
                more = dot(wp[...], jnp.concatenate([hidden[m, i + k] for k in range(4)], axis=1))
                for k in range(0, 4, 2):
                    own = jnp.concatenate([xf[m, pl.ds(i + k + n, VP, stride=R), :] for n in range(2)], axis=1)
                    pn[(r + k) // 2, m * VP:(m + 1) * VP, :] = (own + more[:, k * C:(k + 2) * C]).astype(BF16)
        moved = dot(jnp.concatenate([pn[rp] for rp in range(4)], axis=1), order())
        for t in range(8):
            for m in range(2):
                low = moved[m * VP:m * VP + VH, t * C:(t + 1) * C]
                high = moved[m * VP + VH:(m + 1) * VP, t * C:(t + 1) * C]
                sb[pr, 2 * t, m] = jnp.where(halves, low, half_turn(high)).astype(BF16)
                sb[pr, 2 * t + 1, m] = jnp.where(halves, half_turn(low), high).astype(BF16)

        def send(step, _):
            j = lax.rem(me + step, NM)
            predicted_copy(pr, j, me).start()
            return 0

        lax.fori_loop(1, NM, send, 0)
        rb[pr, me] = sb[pr, me]

    def truth_patches():
        rows = [
            jnp.concatenate([tf[pl.ds(pr * 8 + r, VP, stride=R), :] for r in range(8)], axis=1)
            for pr in range(2)
        ]
        moved = dot(jnp.concatenate(rows, axis=0).astype(BF16), perm[chip])
        for pr in range(2):
            low, high = moved[pr * VP:pr * VP + VH], moved[pr * VP + VH:(pr + 1) * VP]
            first = jnp.where(halves, low, half_turn(high))
            second = jnp.where(halves, half_turn(low), high)
            tp[pr] = jnp.where(core == 0, first, second)

    def square(d):
        d = d * d
        total = d[0:8]
        for k in range(1, VH // 8):
            total = total + d[k * 8:(k + 1) * 8]
        return total

    def gradient_copy(pr, j, source):
        return remote(gb.at[pr, j], gr.at[pr, source], g_send.at[pr, j], g_recv.at[pr, source], member=j)

    def score(pr):
        def arrive(step, _):
            source = lax.rem(me + step, NM)
            predicted_copy(pr, source, source).wait_recv()
            return 0

        lax.fori_loop(1, NM, arrive, 0)

        def widen(source, _):
            for m in range(2):
                pf[source * 2 + m] = rb[pr, source, m].astype(F32)
            return 0

        lax.fori_loop(0, NM, widen, 0)

        def edges(m, _):
            own = pf[m]
            es[pl.ds(pl.multiple_of((NK * MEMBERS + m) * 8, 8), 8), :] = square(own - tp[pr])
            for k in range(NK):
                es[pl.ds(pl.multiple_of((k * MEMBERS + m) * 8, 8), 8), :] = square(own - pf[match[k, m]])
            return 0

        lax.fori_loop(0, MEMBERS, edges, 0)
        count = (NK + 1) * MEMBERS
        total = es[pl.ds(0, count, stride=8), :]
        for k in range(1, 8):
            total = total + es[pl.ds(k, count, stride=8), :]
        for shift in (2, 4, 8, 16, 32, 64):
            total = total + pltpu.roll(total, shift, 1)
        sc[...] = lax.rsqrt(total / (32.0 * V) + 1e-06)

        def member_grad(j):
            for mm in range(2):
                m = j * 2 + mm
                own = pf[m]
                pairs = jnp.zeros((VH, C), F32)
                for k in range(NK):
                    n, n_inv = match[k, m], inverse[m, k]
                    pairs = pairs + (own - pf[n]) * sc[pl.ds(k * MEMBERS + m, 1), :]
                    pairs = pairs + (own - pf[n_inv]) * sc[pl.ds(k * MEMBERS + n_inv, 1), :]
                truth = (own - tp[pr]) * sc[pl.ds(NK * MEMBERS + m, 1), :]
                gb[pr, j, mm] = (truth - pairs * (0.5 / NK)).astype(BF16)

        def member_pair(step, _):
            j = lax.rem(me + step, NM)
            member_grad(j)
            gradient_copy(pr, j, me).start()
            return 0

        lax.fori_loop(1, NM, member_pair, 0)
        member_grad(me)
        gr[pr, me] = gb[pr, me]

    def back_to_rows(pr):
        def gradients_in(step, _):
            source = lax.rem(me + step, NM)
            gradient_copy(pr, source, source).wait_recv()
            return 0

        lax.fori_loop(1, NM, gradients_in, 0)
        parts = []
        for t in range(8):
            rows = []
            for m in range(2):
                first, second = gr[pr, 2 * t, m].astype(F32), gr[pr, 2 * t + 1, m].astype(F32)
                rows.append(jnp.where(halves, first, half_turn(second)))
                rows.append(jnp.where(halves, half_turn(first), second))
            parts.append(jnp.concatenate(rows, axis=0).astype(BF16))
        back = dot_nt(jnp.concatenate(parts, axis=1), order()).astype(BF16)
        for m in range(2):
            for r in range(8):
                gn[m, pr * 8 + r] = back[m * VP:(m + 1) * VP, r * C:(r + 1) * C]

        def hidden_grad(rp, _):
            i = pr * 8 + rp * 2
            for m in range(2):
                dh = dot(wpt[...], pair(gn, m, i))
                for k in range(2):
                    gp[m, i + k + 1] = (dh[:, k * C:(k + 1) * C] * slope[m, i + k]).astype(BF16)
            return 0

        lax.fori_loop(0, 4, hidden_grad, 0)

    def wide(ref, i):
        return jnp.concatenate([ref[m, i + k] for m in range(2) for k in range(8)], axis=1)

    def conv_term(ro, pr):
        term = dot_nt(wide(gp, pr * 8 + 1), wide(x3, pr * 8 + ro))
        acc[ro][:, 0:KP] = term if pr == 0 else acc[ro][:, 0:KP] + term

    def proj_term(pr):
        term = dot_nt(wide(hidden, pr * 8), wide(gn, pr * 8))
        acc[0][:, KP:KP + VP] = term if pr == 0 else acc[0][:, KP:KP + VP] + term

    def core_copy(q):
        return remote(s1[q], r1[q], u_send.at[q], u_recv.at[q], member=me + 1 - 2 * core)

    def core_send(q):
        for c in range(NM // 2):
            base = c * 64 + (1 - core) * 32
            s1[q][c] = acc[q][pl.ds(pl.multiple_of(base, 32), 32), :].astype(BF16)
        core_copy(q).start()

    def sum_copy(place, source):
        return remote(
            s3.at[place], r3.at[source], w_send.at[place], w_recv.at[source],
            member=2 * lax.div(place, NB) + core, band=lax.rem(place, NB),
        )

    def sum_send():
        for q in range(3):
            core_copy(q).wait_recv()
        top = lax.broadcasted_iota(jnp.int32, (8, C), 0) < 4

        def pack(c, _):
            tiles = []
            for q in range(3):
                rows = pl.ds(pl.multiple_of(c * 64 + core * 32, 32), 32)
                value = acc[q][rows, :] + r1[q][c].astype(F32)
                tiles += [value[:, k * C:(k + 1) * C] for k in range(CHUNKS[q] // C)]
            tiles.append(jnp.zeros((32, C), F32))
            for g in range(4):
                parts = [tile[g * 8:(g + 1) * 8] for tile in tiles]
                turned = [pltpu.roll(part, 4, 0) for part in parts]
                first = [jnp.where(top, parts[k], turned[k + 1]) for k in range(0, 8, 2)]
                second = [jnp.where(top, turned[k], parts[k + 1]) for k in range(0, 8, 2)]
                s3[c * NB + 2 * g] = jnp.concatenate(first, axis=0).astype(BF16)
                s3[c * NB + 2 * g + 1] = jnp.concatenate(second, axis=0).astype(BF16)
            return 0

        lax.fori_loop(0, NM // 2, pack, 0)
        pl.semaphore_wait(ready, NB - 1)

        def send(step, _):
            sum_copy(lax.rem(spot + step, GROUP), spot).start()
            return 0

        lax.fori_loop(1, GROUP, send, 0)

    lax.fori_loop(1, 4, forward, 0)
    truth_patches()
    gp_zero = jnp.zeros((H, C), BF16)
    for m in range(2):
        gp[m, 0] = gp_zero
        gp[m, R + 1] = gp_zero
    acc[0][:, KP:] = jnp.zeros((H, 128), F32)
    halo_rows()
    forward(0, 0)
    predict(0)
    lax.fori_loop(4, 8, forward, 0)
    predict(1)
    to_scalars.wait()
    score(0)
    score(1)
    back_to_rows(0)
    proj_term(0)
    for ro in range(3):
        conv_term(ro, 0)
    back_to_rows(1)
    proj_term(1)
    conv_term(0, 1)
    core_send(0)
    conv_term(1, 1)
    core_send(1)
    conv_term(2, 1)
    core_send(2)

    def fold(d):
        def spread(a):
            return (
                jnp.where(lanes[0:a.shape[0]] == C - 1, 0.0, pltpu.roll(a, C - 1, 1)),
                jnp.where(lanes[0:a.shape[0]] == 0, 0.0, pltpu.roll(a, 1, 1)),
            )
        body = spread(d[0:80])[0] + d[80:160] + spread(d[160:240])[1]
        last = spread(d[240:248])[0] + pltpu.roll(d[240:248], 4, 0) + spread(d[248:256])[1]
        return jnp.concatenate([body, last], axis=0)

    for side, ro, row in ((0, 0, 1), (1, 2, R)):
        rows = jnp.concatenate([gp[0, row], gp[1, row]], axis=1)
        d = dot(wt[:, ro * H:(ro + 1) * H], rows)
        for m in range(2):
            edge = jnp.concatenate([fold(d[:, m * C:(m + 1) * C]), jnp.zeros((VP - VQ, C), F32)], axis=0)
            hsb[side, m] = edge.astype(BF16)

    def out_halo(side):
        to = band - 1 if side == 0 else band + 1
        return remote(hsb.at[side], hrb.at[1 - side], o_send.at[side], o_recv.at[1 - side], band=to)

    pl.when(band > 0)(lambda: out_halo(0).start())
    pl.when(band < NB - 1)(lambda: out_halo(1).start())

    def input_grad(m, low, high):
        def step(rp, _):
            i = rp * 2
            rows = jnp.concatenate([pair(gp, m, i + 2 - ro) for ro in range(3)], axis=0)
            d = dot(wt[...], rows)
            for k in range(2):
                value = fold(d[:, k * C:(k + 1) * C]) + gn[m, i + k].astype(F32)[0:VQ]
                of[m, pl.ds(i + k, VQ, stride=R), :] = value
            return 0

        lax.fori_loop(low, high, step, 0)

    sum_send()
    input_grad(0, 0, 8)
    input_grad(1, 0, 8)

    def out_halo_in(side, row):
        remote(hsb.at[1 - side], hrb.at[side], o_send.at[1 - side], o_recv.at[side], band=band).wait_recv()
        for m in range(2):
            of[m, pl.ds(row, VQ, stride=R), :] += hrb[side, m].astype(F32)[0:VQ]

    pl.when(band > 0)(lambda: out_halo_in(0, 0))
    pl.when(band < NB - 1)(lambda: out_halo_in(1, R - 1))

    def write(c, _):
        for m in range(2):
            value = of[m, pl.ds(pl.multiple_of(c * 192, 192), 192), :]
            out[m, pl.ds(c * 12, 12)] = value.reshape(12, R, C).astype(BF16)
        return 0

    lax.fori_loop(0, V // 12, write, 0)

    def sum_take(step, total):
        source = lax.rem(spot + GROUP - step, GROUP)
        sum_copy(source, source).wait_recv()
        return total + r3[source].astype(F32)

    total = lax.fori_loop(1, GROUP, sum_take, s3[spot].astype(F32))
    sums[...] = total * (1.0 / (MEMBERS * NB * R * C) ** 0.5)

    pl.when(band > 0)(lambda: halo(0).wait_send())
    pl.when(band < NB - 1)(lambda: halo(1).wait_send())
    for q in range(3):
        core_copy(q).wait_send()

    def sums_sent(step, _):
        sum_copy(lax.rem(spot + step, GROUP), spot).wait_send()
        return 0

    lax.fori_loop(1, GROUP, sums_sent, 0)
    pl.when(band > 0)(lambda: out_halo(0).wait_send())
    pl.when(band < NB - 1)(lambda: out_halo(1).wait_send())

    def sent(step, _):
        j = lax.rem(me + step, NM)
        for pr in range(2):
            predicted_copy(pr, j, me).wait_send()
            gradient_copy(pr, j, me).wait_send()
        return 0

    lax.fori_loop(1, NM, sent, 0)


def finish(grads, sums, out, conv, proj):
    out[...] = grads[...]
    wide = jnp.concatenate([sums[k * 4:(k + 1) * 4, :] for k in range(7)], axis=1)
    parts = []
    for base in (0, 384, 640):
        for co in range(3):
            parts += [wide[:, base + co * 80:base + (co + 1) * 80], wide[:, base + 240 + co * 4:base + 244 + co * 4]]
    conv[...] = jnp.concatenate(parts, axis=1)
    proj[...] = wide[:, KP:KP + V]


def on_device(states, noise_field, target, w_conv, w_proj, matchings):
    vmem = pl.BlockSpec(memory_space=pltpu.VMEM)
    smem = pl.BlockSpec(memory_space=pltpu.SMEM)
    D = pltpu.SemaphoreType.DMA
    S = pltpu.VMEM
    hbm = pl.BlockSpec(memory_space=pl.ANY)
    scratch = [
        S(states.shape, BF16), S(noise_field.shape, F32), S(target.shape, BF16), S((9 * V, H), BF16), S((V, H), BF16),
        S((8, 8 * C, C), BF16), S((MEMBERS, C), jnp.int32), pltpu.SMEM((MEMBERS, C), jnp.int32), S((9 * V, H), F32), D((7,)),
        S((2, VP * R, C), F32), S((2, R + 2, KP, C), BF16), S((2, 2, VP, C), BF16), S((2, 2, VP, C), BF16),
        S((H, 3 * KP), BF16), S((KP, 3 * H), BF16), S((VP, H), BF16), S((H, VP), BF16),
        S((2, R, H, C), BF16), S((2, R, H, C), F32), S((4, 2 * VP, 2 * C), BF16),
        S((2, NM, 2, VH, C), BF16), S((2, NM, 2, VH, C), BF16), S((MEMBERS, VH, C), F32),
        S((VP * R, C), F32), S((2, VH, C), F32), S(((NK + 1) * MEMBERS * 8, C), F32), S(((NK + 1) * MEMBERS, C), F32),
        S((2, NM, 2, VH, C), BF16), S((2, NM, 2, VH, C), BF16), S((2, R, VP, C), BF16),
        S((2, R + 2, H, C), BF16), S((2, VP * R, C), F32),
        S((2, 2, VP, C), BF16), S((2, 2, VP, C), BF16),
        *[S((H, w), F32) for w in CHUNKS],
        *[S((8, 32, w), BF16) for _ in range(2) for w in CHUNKS],
        S((GROUP, 32, C), BF16), S((GROUP, 32, C), BF16),
        D((2,)), D((2,)), D((2, NM)), D((2, NM)), D((2, NM)), D((2, NM)), D((2,)), D((2,)),
        D((3,)), D((3,)), D((GROUP,)), D((GROUP,)), pltpu.SemaphoreType.REGULAR,
    ]
    grad_states, sums = pl.pallas_call(
        kernel,
        out_shape=(
            jax.ShapeDtypeStruct(states.shape, BF16),
            jax.ShapeDtypeStruct((32, C), F32),
        ),
        in_specs=[hbm] * 6 + [smem, vmem],
        out_specs=(vmem, vmem),
        scratch_shapes=scratch,
        compiler_params=pltpu.CompilerParams(
            collective_id=0, has_side_effects=True, vmem_limit_bytes=60 * 1024 * 1024
        ),
    )(
        states, noise_field, target, w_conv.T, w_proj, jnp.asarray(patch_order()), matchings, matchings,
    )
    grad_states, grad_conv, grad_proj = pl.pallas_call(
        finish,
        out_shape=(
            jax.ShapeDtypeStruct(states.shape, BF16),
            jax.ShapeDtypeStruct((4, 9 * V), F32),
            jax.ShapeDtypeStruct((4, V), F32),
        ),
        in_specs=[vmem] * 2,
        out_specs=(vmem,) * 3,
    )(grad_states, sums)
    return grad_states, grad_conv, grad_proj.T


def solution(mesh):
    return jax.shard_map(
        on_device,
        mesh=mesh,
        in_specs=(
            P("member", None, "band", None),
            P("member", None, "band", None),
            P(None, "band", None),
            P(),
            P(),
            P(),
        ),
        out_specs=(
            P("member", None, "band", None),
            P(("member", "band"), None),
            P(None, ("member", "band")),
        ),
        check_vma=False,
    )
```

```python
import functools

import jax
import jax.numpy as jnp
import ml_dtypes
import numpy as np
from jax import lax
from jax.experimental import pallas as pl
from jax.experimental.pallas import tpu as pltpu
from jax.sharding import PartitionSpec as P

F32, BF16 = jnp.float32, jnp.bfloat16
MESH = pl.DeviceIdType.MESH
V, VP, VQ = 84, 96, 88
VH = VP // 2
R, C, H = 16, 128, 512
NM, NB, NK = 16, 8, 4
GROUP = NM // 2 * NB
MEMBERS = 2 * NM
KP = 256
CHUNKS = (384, 256, 256)


def patch_order():
    table = np.zeros((8, 8 * C, C), ml_dtypes.bfloat16)
    for row in range(8):
        for lon in range(C):
            group, patch, col = lon // 8, lon % 8 // 4, lon % 4
            table[group // 2, row * C + lon, group % 2 * 64 + (row * 4 + col) * 2 + patch] = 1
    return table


def remote(src, dst, send_sem, recv_sem, **device):
    return pltpu.make_async_remote_copy(
        src_ref=src, dst_ref=dst, send_sem=send_sem, recv_sem=recv_sem,
        device_id=device, device_id_type=MESH,
    )


def gelu(x):
    return x * (0.5 + 0.5 * lax.erf(x * 0.7071067811865476))


def gelu_slope(x):
    bell = jnp.exp2((x * x) * (-0.5 * 1.4426950408889634) - 1.3257480647361593)
    return 0.5 + 0.5 * lax.erf(x * 0.7071067811865476) + x * bell


def dot(a, b):
    return jnp.dot(a, b, preferred_element_type=F32)


def dot_nt(a, b):
    return lax.dot_general(a, b, (((1,), (1,)), ((), ())), preferred_element_type=F32)


def kernel(
    states_in, noise_in, target_in, w_conv_in, w_proj_in, perm_in, match, match_v,
    out, sums,
    states, noise, target, w_conv, w_proj, perm, inverse_v, inverse, wide_w, load,
    xf, x3, hs, hb, wf, wt, wp, wpt, hidden, slope, pn, sb, rb, pf, tf, tp, es, sc, gb, gr, gn, gp, of,
    hsb, hrb, a0, a1, a2, s10, s11, s12, r10, r11, r12, s3, r3,
    h_send, h_recv, p_send, p_recv, g_send, g_recv, o_send, o_recv,
    u_send, u_recv, w_send, w_recv, ready,
):
    me, band = lax.axis_index("member"), lax.axis_index("band")
    core, chip = lax.rem(me, 2), lax.div(me, 2)
    lanes = lax.broadcasted_iota(jnp.int32, (VP, C), 1)
    acc = (a0, a1, a2)
    s1, r1 = (s10, s11, s12), (r10, r11, r12)
    spot = chip * NB + band

    halves = lax.broadcasted_iota(jnp.int32, (VH, C), 1) < 64
    loads = [
        pltpu.make_async_copy(a, b, load.at[k])
        for k, (a, b) in enumerate((
            (w_conv_in, w_conv), (w_proj_in, w_proj), (noise_in, noise), (states_in, states),
            (target_in, target), (perm_in, perm),
        ))
    ]
    for copy in loads:
        copy.start()
    barrier = pltpu.get_barrier_semaphore()

    def greet_member(step, _):
        pl.semaphore_signal(barrier, inc=1, device_id={"member": lax.rem(me + step, NM)}, device_id_type=MESH)
        return 0

    def greet_band(step, _):
        pl.semaphore_signal(barrier, inc=1, device_id={"band": lax.rem(band + step, NB)}, device_id_type=MESH)
        return 0

    lax.fori_loop(1, NM, greet_member, 0)
    lax.fori_loop(1, NB, greet_band, 0)

    to_member = lax.broadcasted_iota(jnp.int32, (MEMBERS, MEMBERS), 0)
    number = lax.broadcasted_iota(jnp.int32, (MEMBERS, MEMBERS), 1)
    column = lax.broadcasted_iota(jnp.int32, (MEMBERS, C), 1)
    table = jnp.zeros((MEMBERS, C), jnp.int32)
    for k in range(NK):
        hit = jnp.where(match_v[k:k + 1, :] == to_member, number, 0)
        table = jnp.where(column == k, jnp.max(hit, axis=1, keepdims=True), table)
    inverse_v[...] = table
    to_scalars = pltpu.make_async_copy(inverse_v, inverse, load.at[6])
    to_scalars.start()

    for copy in loads[:2]:
        copy.wait()
    wide_w[...] = w_conv[...].astype(F32)
    for ro in range(3):
        base = ro * 3 * V
        parts = [wide_w[base + co * V:base + co * V + 80, :] for co in range(3)]
        parts += [wide_w[base + co * V + 80:base + (co + 1) * V, :] for co in range(3)]
        w_part = jnp.concatenate(parts + [jnp.zeros((KP - 3 * V, H), F32)], axis=0)
        wt[:, ro * H:(ro + 1) * H] = w_part.astype(BF16)
        wf[:, ro * KP:(ro + 1) * KP] = w_part.T.astype(BF16)
    w_pad = jnp.concatenate([w_proj[...].astype(F32), jnp.zeros((VP - V, H), F32)], axis=0)
    wp[...] = w_pad.astype(BF16)
    wpt[...] = w_pad.T.astype(BF16)

    for copy in loads[2:5]:
        copy.wait()
    def add_inputs(c, _):
        part = pl.ds(c * 12, 12)
        to = pl.ds(pl.multiple_of(c * 192, 192), 192)
        for m in range(2):
            value = (states[m, part].astype(F32) + noise[m, part]).astype(BF16).astype(F32)
            xf[m, to, :] = value.reshape(192, C)
        tf[to, :] = target[part].astype(F32).reshape(192, C)
        return 0

    lax.fori_loop(0, V // 12, add_inputs, 0)
    for m in range(2):
        xf[m, V * R:, :] = jnp.zeros(((VP - V) * R, C), F32)
    tf[V * R:, :] = jnp.zeros(((VP - V) * R, C), F32)

    for side, row in ((0, 0), (1, R - 1)):
        for m in range(2):
            hs[side, m] = xf[m, pl.ds(row, VP, stride=R), :].astype(BF16)

    def put_row(m, slot, x):
        left = jnp.where(lanes == 0, 0.0, pltpu.roll(x, 1, 1))
        right = jnp.where(lanes == C - 1, 0.0, pltpu.roll(x, C - 1, 1))
        x3[m, slot, 0:80, :] = left[0:80].astype(BF16)
        x3[m, slot, 80:160, :] = x[0:80].astype(BF16)
        x3[m, slot, 160:240, :] = right[0:80].astype(BF16)
        first = left[80:88] + pltpu.roll(x[80:88], 4, 0)
        x3[m, slot, 240:256, :] = jnp.concatenate([first, right[80:88]], axis=0).astype(BF16)

    def build(r, _):
        for m in range(2):
            put_row(m, r + 1, xf[m, pl.ds(r, VP, stride=R), :])
        return 0

    lax.fori_loop(0, R, build, 0)

    loads[5].wait()
    pl.semaphore_wait(barrier, NM + NB - 2)

    def all_here(step, _):
        pl.semaphore_signal(ready, inc=1, device_id={"band": lax.rem(band + step, NB)}, device_id_type=MESH)
        return 0

    lax.fori_loop(1, NB, all_here, 0)
    def halo(side):
        to = band - 1 if side == 0 else band + 1
        return remote(hs.at[side], hb.at[1 - side], h_send.at[side], h_recv.at[1 - side], band=to)

    pl.when(band > 0)(lambda: halo(0).start())
    pl.when(band < NB - 1)(lambda: halo(1).start())

    def halo_in(side, slot):
        remote(hs.at[1 - side], hb.at[side], h_send.at[1 - side], h_recv.at[side], band=band).wait_recv()
        for m in range(2):
            put_row(m, slot, hb[side, m].astype(F32))

    def no_halo(slot):
        for m in range(2):
            x3[m, slot] = jnp.zeros((KP, C), BF16)

    def halo_rows():
        pl.when(band > 0)(lambda: halo_in(0, 0))
        pl.when(band == 0)(lambda: no_halo(0))
        pl.when(band < NB - 1)(lambda: halo_in(1, R + 1))
        pl.when(band == NB - 1)(lambda: no_halo(R + 1))

    def pair(ref, m, i):
        return jnp.concatenate([ref[m, i], ref[m, i + 1]], axis=1)

    def order():
        return jnp.concatenate([perm[t] for t in range(8)], axis=1)

    def half_turn(a):
        return pltpu.roll(a, 64, 1)

    def predicted_copy(pr, j, source):
        return remote(sb.at[pr, j], rb.at[pr, source], p_send.at[pr, j], p_recv.at[pr, source], member=j)

    def forward(rp, _):
        i = rp * 2
        for m in range(2):
            columns = jnp.concatenate([pair(x3, m, i + ro) for ro in range(3)], axis=0)
            for part in range(0, H, H // 2):
                rows = slice(part, part + H // 2)
                pre = dot(wf[rows, :], columns)
                value = gelu(pre).astype(BF16)
                for k in range(2):
                    hidden[m, i + k, rows, :] = value[:, k * C:(k + 1) * C]
                    slope[m, i + k, rows, :] = pre[:, k * C:(k + 1) * C]
        return 0

    def slopes(pr):
        def step(r, _):
            for m in range(2):
                slope[m, pr * 8 + r] = gelu_slope(slope[m, pr * 8 + r])
            return 0

        lax.fori_loop(0, 8, step, 0)

    def predict(pr):
        for m in range(2):
            for r in range(0, 8, 4):
                i = pr * 8 + r
                more = dot(wp[...], jnp.concatenate([hidden[m, i + k] for k in range(4)], axis=1))
                for k in range(0, 4, 2):
                    own = jnp.concatenate([xf[m, pl.ds(i + k + n, VP, stride=R), :] for n in range(2)], axis=1)
                    pn[(r + k) // 2, m * VP:(m + 1) * VP, :] = (own + more[:, k * C:(k + 2) * C]).astype(BF16)
        moved = dot(jnp.concatenate([pn[rp] for rp in range(4)], axis=1), order())
        for t in range(8):
            for m in range(2):
                low = moved[m * VP:m * VP + VH, t * C:(t + 1) * C]
                high = moved[m * VP + VH:(m + 1) * VP, t * C:(t + 1) * C]
                sb[pr, 2 * t, m] = jnp.where(halves, low, half_turn(high)).astype(BF16)
                sb[pr, 2 * t + 1, m] = jnp.where(halves, half_turn(low), high).astype(BF16)

        def send(step, _):
            j = lax.rem(me + step, NM)
            predicted_copy(pr, j, me).start()
            return 0

        lax.fori_loop(1, NM, send, 0)
        rb[pr, me] = sb[pr, me]

    def truth_patches():
        rows = [
            jnp.concatenate([tf[pl.ds(pr * 8 + r, VP, stride=R), :] for r in range(8)], axis=1)
            for pr in range(2)
        ]
        moved = dot(jnp.concatenate(rows, axis=0).astype(BF16), perm[chip])
        for pr in range(2):
            low, high = moved[pr * VP:pr * VP + VH], moved[pr * VP + VH:(pr + 1) * VP]
            first = jnp.where(halves, low, half_turn(high))
            second = jnp.where(halves, half_turn(low), high)
            tp[pr] = jnp.where(core == 0, first, second)

    def square(d):
        d = d * d
        total = d[0:8]
        for k in range(1, VH // 8):
            total = total + d[k * 8:(k + 1) * 8]
        return total

    def gradient_copy(pr, j, source):
        return remote(gb.at[pr, j], gr.at[pr, source], g_send.at[pr, j], g_recv.at[pr, source], member=j)

    def score(pr):
        def arrive(step, _):
            source = lax.rem(me + step, NM)
            predicted_copy(pr, source, source).wait_recv()
            return 0

        lax.fori_loop(1, NM, arrive, 0)

        def widen(source, _):
            for m in range(2):
                pf[source * 2 + m] = rb[pr, source, m].astype(F32)
            return 0

        lax.fori_loop(0, NM, widen, 0)

        def edges(m, _):
            own = pf[m]
            es[pl.ds(pl.multiple_of((NK * MEMBERS + m) * 8, 8), 8), :] = square(own - tp[pr])
            for k in range(NK):
                es[pl.ds(pl.multiple_of((k * MEMBERS + m) * 8, 8), 8), :] = square(own - pf[match[k, m]])
            return 0

        lax.fori_loop(0, MEMBERS, edges, 0)
        count = (NK + 1) * MEMBERS
        total = es[pl.ds(0, count, stride=8), :]
        for k in range(1, 8):
            total = total + es[pl.ds(k, count, stride=8), :]
        for shift in (2, 4, 8, 16, 32, 64):
            total = total + pltpu.roll(total, shift, 1)
        sc[...] = lax.rsqrt(total / (32.0 * V) + 1e-06)

        def member_grad(j):
            for mm in range(2):
                m = j * 2 + mm
                own = pf[m]
                pairs = jnp.zeros((VH, C), F32)
                for k in range(NK):
                    n, n_inv = match[k, m], inverse[m, k]
                    pairs = pairs + (own - pf[n]) * sc[pl.ds(k * MEMBERS + m, 1), :]
                    pairs = pairs + (own - pf[n_inv]) * sc[pl.ds(k * MEMBERS + n_inv, 1), :]
                truth = (own - tp[pr]) * sc[pl.ds(NK * MEMBERS + m, 1), :]
                gb[pr, j, mm] = (truth - pairs * (0.5 / NK)).astype(BF16)

        def member_pair(step, _):
            j = lax.rem(me + step, NM)
            member_grad(j)
            gradient_copy(pr, j, me).start()
            return 0

        lax.fori_loop(1, NM, member_pair, 0)
        member_grad(me)
        gr[pr, me] = gb[pr, me]

    def back_to_rows(pr):
        def gradients_in(step, _):
            source = lax.rem(me + step, NM)
            gradient_copy(pr, source, source).wait_recv()
            return 0

        lax.fori_loop(1, NM, gradients_in, 0)
        parts = []
        for t in range(8):
            rows = []
            for m in range(2):
                first, second = gr[pr, 2 * t, m].astype(F32), gr[pr, 2 * t + 1, m].astype(F32)
                rows.append(jnp.where(halves, first, half_turn(second)))
                rows.append(jnp.where(halves, half_turn(first), second))
            parts.append(jnp.concatenate(rows, axis=0).astype(BF16))
        back = dot_nt(jnp.concatenate(parts, axis=1), order()).astype(BF16)
        for m in range(2):
            for r in range(8):
                gn[m, pr * 8 + r] = back[m * VP:(m + 1) * VP, r * C:(r + 1) * C]

        def hidden_grad(rp, _):
            i = pr * 8 + rp * 2
            for m in range(2):
                dh = dot(wpt[...], pair(gn, m, i))
                for k in range(2):
                    gp[m, i + k + 1] = (dh[:, k * C:(k + 1) * C] * slope[m, i + k]).astype(BF16)
            return 0

        lax.fori_loop(0, 4, hidden_grad, 0)

    def wide(ref, i):
        return jnp.concatenate([ref[m, i + k] for m in range(2) for k in range(8)], axis=1)

    def conv_term(ro, pr):
        term = dot_nt(wide(gp, pr * 8 + 1), wide(x3, pr * 8 + ro))
        acc[ro][:, 0:KP] = term if pr == 0 else acc[ro][:, 0:KP] + term

    def proj_term(pr):
        term = dot_nt(wide(hidden, pr * 8), wide(gn, pr * 8))
        acc[0][:, KP:KP + VP] = term if pr == 0 else acc[0][:, KP:KP + VP] + term

    def core_copy(q):
        return remote(s1[q], r1[q], u_send.at[q], u_recv.at[q], member=me + 1 - 2 * core)

    def core_send(q):
        for c in range(NM // 2):
            base = c * 64 + (1 - core) * 32
            s1[q][c] = acc[q][pl.ds(pl.multiple_of(base, 32), 32), :].astype(BF16)
        core_copy(q).start()

    def sum_copy(place, source):
        return remote(
            s3.at[place], r3.at[source], w_send.at[place], w_recv.at[source],
            member=2 * lax.div(place, NB) + core, band=lax.rem(place, NB),
        )

    def sum_send():
        for q in range(3):
            core_copy(q).wait_recv()
        top = lax.broadcasted_iota(jnp.int32, (8, C), 0) < 4

        def pack(c, _):
            tiles = []
            for q in range(3):
                rows = pl.ds(pl.multiple_of(c * 64 + core * 32, 32), 32)
                value = acc[q][rows, :] + r1[q][c].astype(F32)
                tiles += [value[:, k * C:(k + 1) * C] for k in range(CHUNKS[q] // C)]
            tiles.append(jnp.zeros((32, C), F32))
            for g in range(4):
                parts = [tile[g * 8:(g + 1) * 8] for tile in tiles]
                turned = [pltpu.roll(part, 4, 0) for part in parts]
                first = [jnp.where(top, parts[k], turned[k + 1]) for k in range(0, 8, 2)]
                second = [jnp.where(top, turned[k], parts[k + 1]) for k in range(0, 8, 2)]
                s3[c * NB + 2 * g] = jnp.concatenate(first, axis=0).astype(BF16)
                s3[c * NB + 2 * g + 1] = jnp.concatenate(second, axis=0).astype(BF16)
            return 0

        lax.fori_loop(0, NM // 2, pack, 0)
        pl.semaphore_wait(ready, NB - 1)

        def send(step, _):
            sum_copy(lax.rem(spot + step, GROUP), spot).start()
            return 0

        lax.fori_loop(1, GROUP, send, 0)

    lax.fori_loop(1, 4, forward, 0)
    halo_rows()
    forward(0, 0)
    predict(0)
    lax.fori_loop(4, 8, forward, 0)
    predict(1)
    truth_patches()
    gp_zero = jnp.zeros((H, C), BF16)
    for m in range(2):
        gp[m, 0] = gp_zero
        gp[m, R + 1] = gp_zero
    acc[0][:, KP:] = jnp.zeros((H, 128), F32)
    to_scalars.wait()
    score(0)
    slopes(0)
    score(1)
    slopes(1)
    back_to_rows(0)
    proj_term(0)
    for ro in range(3):
        conv_term(ro, 0)
    back_to_rows(1)
    proj_term(1)
    conv_term(0, 1)
    core_send(0)
    conv_term(1, 1)
    core_send(1)
    conv_term(2, 1)
    core_send(2)

    def fold(d):
        def spread(a):
            return (
                jnp.where(lanes[0:a.shape[0]] == C - 1, 0.0, pltpu.roll(a, C - 1, 1)),
                jnp.where(lanes[0:a.shape[0]] == 0, 0.0, pltpu.roll(a, 1, 1)),
            )
        body = spread(d[0:80])[0] + d[80:160] + spread(d[160:240])[1]
        last = spread(d[240:248])[0] + pltpu.roll(d[240:248], 4, 0) + spread(d[248:256])[1]
        return jnp.concatenate([body, last], axis=0)

    for side, ro, row in ((0, 0, 1), (1, 2, R)):
        rows = jnp.concatenate([gp[0, row], gp[1, row]], axis=1)
        d = dot(wt[:, ro * H:(ro + 1) * H], rows)
        for m in range(2):
            edge = jnp.concatenate([fold(d[:, m * C:(m + 1) * C]), jnp.zeros((VP - VQ, C), F32)], axis=0)
            hsb[side, m] = edge.astype(BF16)

    def out_halo(side):
        to = band - 1 if side == 0 else band + 1
        return remote(hsb.at[side], hrb.at[1 - side], o_send.at[side], o_recv.at[1 - side], band=to)

    pl.when(band > 0)(lambda: out_halo(0).start())
    pl.when(band < NB - 1)(lambda: out_halo(1).start())

    def input_grad(m, low, high):
        def step(rp, _):
            i = rp * 2
            rows = jnp.concatenate([pair(gp, m, i + 2 - ro) for ro in range(3)], axis=0)
            d = dot(wt[...], rows)
            for k in range(2):
                value = fold(d[:, k * C:(k + 1) * C]) + gn[m, i + k].astype(F32)[0:VQ]
                of[m, pl.ds(i + k, VQ, stride=R), :] = value
            return 0

        lax.fori_loop(low, high, step, 0)

    sum_send()
    input_grad(0, 0, 8)
    input_grad(1, 0, 8)

    def out_halo_in(side, row):
        remote(hsb.at[1 - side], hrb.at[side], o_send.at[1 - side], o_recv.at[side], band=band).wait_recv()
        for m in range(2):
            of[m, pl.ds(row, VQ, stride=R), :] += hrb[side, m].astype(F32)[0:VQ]

    pl.when(band > 0)(lambda: out_halo_in(0, 0))
    pl.when(band < NB - 1)(lambda: out_halo_in(1, R - 1))

    def write(c, _):
        for m in range(2):
            value = of[m, pl.ds(pl.multiple_of(c * 192, 192), 192), :]
            out[m, pl.ds(c * 12, 12)] = value.reshape(12, R, C).astype(BF16)
        return 0

    lax.fori_loop(0, V // 12, write, 0)

    def sum_take(step, total):
        source = lax.rem(spot + GROUP - step, GROUP)
        sum_copy(source, source).wait_recv()
        return total + r3[source].astype(F32)

    total = lax.fori_loop(1, GROUP, sum_take, s3[spot].astype(F32))
    sums[...] = total * (1.0 / (MEMBERS * NB * R * C) ** 0.5)

    pl.when(band > 0)(lambda: halo(0).wait_send())
    pl.when(band < NB - 1)(lambda: halo(1).wait_send())
    for q in range(3):
        core_copy(q).wait_send()

    def sums_sent(step, _):
        sum_copy(lax.rem(spot + step, GROUP), spot).wait_send()
        return 0

    lax.fori_loop(1, GROUP, sums_sent, 0)
    pl.when(band > 0)(lambda: out_halo(0).wait_send())
    pl.when(band < NB - 1)(lambda: out_halo(1).wait_send())

    def sent(step, _):
        j = lax.rem(me + step, NM)
        for pr in range(2):
            predicted_copy(pr, j, me).wait_send()
            gradient_copy(pr, j, me).wait_send()
        return 0

    lax.fori_loop(1, NM, sent, 0)


def finish(grads, sums, out, conv, proj):
    out[...] = grads[...]
    wide = jnp.concatenate([sums[k * 4:(k + 1) * 4, :] for k in range(7)], axis=1)
    parts = []
    for base in (0, 384, 640):
        for co in range(3):
            parts += [wide[:, base + co * 80:base + (co + 1) * 80], wide[:, base + 240 + co * 4:base + 244 + co * 4]]
    conv[...] = jnp.concatenate(parts, axis=1)
    proj[...] = wide[:, KP:KP + V]


def on_device(states, noise_field, target, w_conv, w_proj, matchings):
    vmem = pl.BlockSpec(memory_space=pltpu.VMEM)
    smem = pl.BlockSpec(memory_space=pltpu.SMEM)
    D = pltpu.SemaphoreType.DMA
    S = pltpu.VMEM
    hbm = pl.BlockSpec(memory_space=pl.ANY)
    scratch = [
        S(states.shape, BF16), S(noise_field.shape, F32), S(target.shape, BF16), S((9 * V, H), BF16), S((V, H), BF16),
        S((8, 8 * C, C), BF16), S((MEMBERS, C), jnp.int32), pltpu.SMEM((MEMBERS, C), jnp.int32), S((9 * V, H), F32), D((7,)),
        S((2, VP * R, C), F32), S((2, R + 2, KP, C), BF16), S((2, 2, VP, C), BF16), S((2, 2, VP, C), BF16),
        S((H, 3 * KP), BF16), S((KP, 3 * H), BF16), S((VP, H), BF16), S((H, VP), BF16),
        S((2, R, H, C), BF16), S((2, R, H, C), F32), S((4, 2 * VP, 2 * C), BF16),
        S((2, NM, 2, VH, C), BF16), S((2, NM, 2, VH, C), BF16), S((MEMBERS, VH, C), F32),
        S((VP * R, C), F32), S((2, VH, C), F32), S(((NK + 1) * MEMBERS * 8, C), F32), S(((NK + 1) * MEMBERS, C), F32),
        S((2, NM, 2, VH, C), BF16), S((2, NM, 2, VH, C), BF16), S((2, R, VP, C), BF16),
        S((2, R + 2, H, C), BF16), S((2, VP * R, C), F32),
        S((2, 2, VP, C), BF16), S((2, 2, VP, C), BF16),
        *[S((H, w), F32) for w in CHUNKS],
        *[S((8, 32, w), BF16) for _ in range(2) for w in CHUNKS],
        S((GROUP, 32, C), BF16), S((GROUP, 32, C), BF16),
        D((2,)), D((2,)), D((2, NM)), D((2, NM)), D((2, NM)), D((2, NM)), D((2,)), D((2,)),
        D((3,)), D((3,)), D((GROUP,)), D((GROUP,)), pltpu.SemaphoreType.REGULAR,
    ]
    grad_states, sums = pl.pallas_call(
        kernel,
        out_shape=(
            jax.ShapeDtypeStruct(states.shape, BF16),
            jax.ShapeDtypeStruct((32, C), F32),
        ),
        in_specs=[hbm] * 6 + [smem, vmem],
        out_specs=(vmem, vmem),
        scratch_shapes=scratch,
        compiler_params=pltpu.CompilerParams(
            collective_id=0, has_side_effects=True, vmem_limit_bytes=60 * 1024 * 1024
        ),
    )(
        states, noise_field, target, w_conv.T, w_proj, jnp.asarray(patch_order()), matchings, matchings,
    )
    grad_states, grad_conv, grad_proj = pl.pallas_call(
        finish,
        out_shape=(
            jax.ShapeDtypeStruct(states.shape, BF16),
            jax.ShapeDtypeStruct((4, 9 * V), F32),
            jax.ShapeDtypeStruct((4, V), F32),
        ),
        in_specs=[vmem] * 2,
        out_specs=(vmem,) * 3,
    )(grad_states, sums)
    return grad_states, grad_conv, grad_proj.T


def solution(mesh):
    return jax.shard_map(
        on_device,
        mesh=mesh,
        in_specs=(
            P("member", None, "band", None),
            P("member", None, "band", None),
            P(None, "band", None),
            P(),
            P(),
            P(),
        ),
        out_specs=(
            P("member", None, "band", None),
            P(("member", "band"), None),
            P(None, ("member", "band")),
        ),
        check_vma=False,
    )
```

```python
import functools

import jax
import jax.numpy as jnp
import ml_dtypes
import numpy as np
from jax import lax
from jax.experimental import pallas as pl
from jax.experimental.pallas import tpu as pltpu
from jax.sharding import PartitionSpec as P

F32, BF16 = jnp.float32, jnp.bfloat16
MESH = pl.DeviceIdType.MESH
V, VP, VQ = 84, 96, 88
VH = VP // 2
R, C, H = 16, 128, 512
NM, NB, NK = 16, 8, 4
GROUP = NM // 2 * NB
MEMBERS = 2 * NM
KP = 256
CHUNKS = (384, 256, 256)


def patch_order():
    table = np.zeros((8, 8 * C, C), ml_dtypes.bfloat16)
    for row in range(8):
        for lon in range(C):
            group, patch, col = lon // 8, lon % 8 // 4, lon % 4
            table[group // 2, row * C + lon, group % 2 * 64 + (row * 4 + col) * 2 + patch] = 1
    return table


def remote(src, dst, send_sem, recv_sem, **device):
    return pltpu.make_async_remote_copy(
        src_ref=src, dst_ref=dst, send_sem=send_sem, recv_sem=recv_sem,
        device_id=device, device_id_type=MESH,
    )


def gelu(x):
    return x * (0.5 + 0.5 * lax.erf(x * 0.7071067811865476))


def gelu_slope(x):
    bell = jnp.exp2((x * x) * (-0.5 * 1.4426950408889634) - 1.3257480647361593)
    return 0.5 + 0.5 * lax.erf(x * 0.7071067811865476) + x * bell


def dot(a, b):
    return jnp.dot(a, b, preferred_element_type=F32)


def dot_nt(a, b):
    return lax.dot_general(a, b, (((1,), (1,)), ((), ())), preferred_element_type=F32)


def kernel(
    states_in, noise_in, target_in, w_conv_in, w_proj_in, perm_in, match, match_v,
    out, sums,
    states, noise, target, w_conv, w_proj, perm, inverse_v, inverse, wide_w, load,
    xf, x3, hs, hb, wf, wt, wp, wpt, hidden, slope, pn, sb, rb, pf, tf, tp, es, sc, gb, gr, gn, gp, of,
    hsb, hrb, a0, a1, a2, s10, s11, s12, r10, r11, r12, s3, r3,
    h_send, h_recv, p_send, p_recv, g_send, g_recv, o_send, o_recv,
    u_send, u_recv, w_send, w_recv, ready,
):
    me, band = lax.axis_index("member"), lax.axis_index("band")
    core, chip = lax.rem(me, 2), lax.div(me, 2)
    lanes = lax.broadcasted_iota(jnp.int32, (VP, C), 1)
    acc = (a0, a1, a2)
    s1, r1 = (s10, s11, s12), (r10, r11, r12)
    spot = chip * NB + band

    halves = lax.broadcasted_iota(jnp.int32, (VH, C), 1) < 64
    loads = [
        pltpu.make_async_copy(a, b, load.at[k])
        for k, (a, b) in enumerate((
            (w_conv_in, w_conv), (w_proj_in, w_proj), (noise_in, noise), (states_in, states),
            (target_in, target), (perm_in, perm),
        ))
    ]
    for copy in loads:
        copy.start()
    barrier = pltpu.get_barrier_semaphore()

    def greet_member(step, _):
        pl.semaphore_signal(barrier, inc=1, device_id={"member": lax.rem(me + step, NM)}, device_id_type=MESH)
        return 0

    def greet_band(step, _):
        pl.semaphore_signal(barrier, inc=1, device_id={"band": lax.rem(band + step, NB)}, device_id_type=MESH)
        return 0

    lax.fori_loop(1, NM, greet_member, 0)
    lax.fori_loop(1, NB, greet_band, 0)

    to_member = lax.broadcasted_iota(jnp.int32, (MEMBERS, MEMBERS), 0)
    number = lax.broadcasted_iota(jnp.int32, (MEMBERS, MEMBERS), 1)
    column = lax.broadcasted_iota(jnp.int32, (MEMBERS, C), 1)
    table = jnp.zeros((MEMBERS, C), jnp.int32)
    for k in range(NK):
        hit = jnp.where(match_v[k:k + 1, :] == to_member, number, 0)
        table = jnp.where(column == k, jnp.max(hit, axis=1, keepdims=True), table)
    inverse_v[...] = table
    to_scalars = pltpu.make_async_copy(inverse_v, inverse, load.at[6])
    to_scalars.start()

    for copy in loads[:2]:
        copy.wait()
    wide_w[...] = w_conv[...].astype(F32)
    for ro in range(3):
        base = ro * 3 * V
        parts = [wide_w[base + co * V:base + co * V + 80, :] for co in range(3)]
        parts += [wide_w[base + co * V + 80:base + (co + 1) * V, :] for co in range(3)]
        w_part = jnp.concatenate(parts + [jnp.zeros((KP - 3 * V, H), F32)], axis=0)
        wt[:, ro * H:(ro + 1) * H] = w_part.astype(BF16)
        wf[:, ro * KP:(ro + 1) * KP] = w_part.T.astype(BF16)
    w_pad = jnp.concatenate([w_proj[...].astype(F32), jnp.zeros((VP - V, H), F32)], axis=0)
    wp[...] = w_pad.astype(BF16)
    wpt[...] = w_pad.T.astype(BF16)

    for copy in loads[2:5]:
        copy.wait()
    def add_inputs(c, _):
        part = pl.ds(c * 12, 12)
        to = pl.ds(pl.multiple_of(c * 192, 192), 192)
        for m in range(2):
            value = (states[m, part].astype(F32) + noise[m, part]).astype(BF16).astype(F32)
            xf[m, to, :] = value.reshape(192, C)
        tf[to, :] = target[part].astype(F32).reshape(192, C)
        return 0

    lax.fori_loop(0, V // 12, add_inputs, 0)
    for m in range(2):
        xf[m, V * R:, :] = jnp.zeros(((VP - V) * R, C), F32)
    tf[V * R:, :] = jnp.zeros(((VP - V) * R, C), F32)

    for side, row in ((0, 0), (1, R - 1)):
        for m in range(2):
            hs[side, m] = xf[m, pl.ds(row, VP, stride=R), :].astype(BF16)

    def put_row(m, slot, x):
        left = jnp.where(lanes == 0, 0.0, pltpu.roll(x, 1, 1))
        right = jnp.where(lanes == C - 1, 0.0, pltpu.roll(x, C - 1, 1))
        x3[m, slot, 0:80, :] = left[0:80].astype(BF16)
        x3[m, slot, 80:160, :] = x[0:80].astype(BF16)
        x3[m, slot, 160:240, :] = right[0:80].astype(BF16)
        first = left[80:88] + pltpu.roll(x[80:88], 4, 0)
        x3[m, slot, 240:256, :] = jnp.concatenate([first, right[80:88]], axis=0).astype(BF16)

    def build(r, _):
        for m in range(2):
            put_row(m, r + 1, xf[m, pl.ds(r, VP, stride=R), :])
        return 0

    lax.fori_loop(0, R, build, 0)

    loads[5].wait()
    pl.semaphore_wait(barrier, NM + NB - 2)

    def all_here(step, _):
        pl.semaphore_signal(ready, inc=1, device_id={"band": lax.rem(band + step, NB)}, device_id_type=MESH)
        return 0

    lax.fori_loop(1, NB, all_here, 0)
    def halo(side):
        to = band - 1 if side == 0 else band + 1
        return remote(hs.at[side], hb.at[1 - side], h_send.at[side], h_recv.at[1 - side], band=to)

    pl.when(band > 0)(lambda: halo(0).start())
    pl.when(band < NB - 1)(lambda: halo(1).start())

    def halo_in(side, slot):
        remote(hs.at[1 - side], hb.at[side], h_send.at[1 - side], h_recv.at[side], band=band).wait_recv()
        for m in range(2):
            put_row(m, slot, hb[side, m].astype(F32))

    def no_halo(slot):
        for m in range(2):
            x3[m, slot] = jnp.zeros((KP, C), BF16)

    def halo_rows():
        pl.when(band > 0)(lambda: halo_in(0, 0))
        pl.when(band == 0)(lambda: no_halo(0))
        pl.when(band < NB - 1)(lambda: halo_in(1, R + 1))
        pl.when(band == NB - 1)(lambda: no_halo(R + 1))

    def pair(ref, m, i):
        return jnp.concatenate([ref[m, i], ref[m, i + 1]], axis=1)

    def order():
        return jnp.concatenate([perm[t] for t in range(8)], axis=1)

    def half_turn(a):
        return pltpu.roll(a, 64, 1)

    def predicted_copy(pr, j, source):
        return remote(sb.at[pr, j], rb.at[pr, source], p_send.at[pr, j], p_recv.at[pr, source], member=j)

    def forward(rp, _):
        i = rp * 2
        for m in range(2):
            columns = jnp.concatenate([pair(x3, m, i + ro) for ro in range(3)], axis=0)
            for part in range(0, H, H // 2):
                rows = slice(part, part + H // 2)
                pre = dot(wf[rows, :], columns)
                value = gelu(pre).astype(BF16)
                for k in range(2):
                    hidden[m, i + k, rows, :] = value[:, k * C:(k + 1) * C]
                    slope[m, i + k, rows, :] = pre[:, k * C:(k + 1) * C]
        return 0

    def slopes(pr):
        def step(r, _):
            for m in range(2):
                slope[m, pr * 8 + r] = gelu_slope(slope[m, pr * 8 + r])
            return 0

        lax.fori_loop(0, 8, step, 0)

    def predict(pr):
        for m in range(2):
            for r in range(0, 8, 4):
                i = pr * 8 + r
                more = dot(wp[...], jnp.concatenate([hidden[m, i + k] for k in range(4)], axis=1))
                for k in range(0, 4, 2):
                    own = jnp.concatenate([xf[m, pl.ds(i + k + n, VP, stride=R), :] for n in range(2)], axis=1)
                    pn[(r + k) // 2, m * VP:(m + 1) * VP, :] = (own + more[:, k * C:(k + 2) * C]).astype(BF16)
        moved = dot(jnp.concatenate([pn[rp] for rp in range(4)], axis=1), order())
        for t in range(8):
            for m in range(2):
                low = moved[m * VP:m * VP + VH, t * C:(t + 1) * C]
                high = moved[m * VP + VH:(m + 1) * VP, t * C:(t + 1) * C]
                sb[pr, 2 * t, m] = jnp.where(halves, low, half_turn(high)).astype(BF16)
                sb[pr, 2 * t + 1, m] = jnp.where(halves, half_turn(low), high).astype(BF16)

        def send(step, _):
            j = lax.rem(me + step, NM)
            predicted_copy(pr, j, me).start()
            return 0

        lax.fori_loop(1, NM, send, 0)
        rb[pr, me] = sb[pr, me]

    def truth_patches():
        rows = [
            jnp.concatenate([tf[pl.ds(pr * 8 + r, VP, stride=R), :] for r in range(8)], axis=1)
            for pr in range(2)
        ]
        moved = dot(jnp.concatenate(rows, axis=0).astype(BF16), perm[chip])
        for pr in range(2):
            low, high = moved[pr * VP:pr * VP + VH], moved[pr * VP + VH:(pr + 1) * VP]
            first = jnp.where(halves, low, half_turn(high))
            second = jnp.where(halves, half_turn(low), high)
            tp[pr] = jnp.where(core == 0, first, second)

    def square(d):
        d = d * d
        total = d[0:8]
        for k in range(1, VH // 8):
            total = total + d[k * 8:(k + 1) * 8]
        return total

    def gradient_copy(pr, j, source):
        return remote(gb.at[pr, j], gr.at[pr, source], g_send.at[pr, j], g_recv.at[pr, source], member=j)

    def score(pr):
        def arrive(step, _):
            source = lax.rem(me + step, NM)
            predicted_copy(pr, source, source).wait_recv()
            return 0

        lax.fori_loop(1, NM, arrive, 0)

        def widen(source, _):
            for m in range(2):
                pf[source * 2 + m] = rb[pr, source, m].astype(F32)
            return 0

        lax.fori_loop(0, NM, widen, 0)

        def edges(m, _):
            own = pf[m]
            es[pl.ds(pl.multiple_of((NK * MEMBERS + m) * 8, 8), 8), :] = square(own - tp[pr])
            for k in range(NK):
                es[pl.ds(pl.multiple_of((k * MEMBERS + m) * 8, 8), 8), :] = square(own - pf[match[k, m]])
            return 0

        lax.fori_loop(0, MEMBERS, edges, 0)
        count = (NK + 1) * MEMBERS
        total = es[pl.ds(0, count, stride=8), :]
        for k in range(1, 8):
            total = total + es[pl.ds(k, count, stride=8), :]
        for shift in (2, 4, 8, 16, 32, 64):
            total = total + pltpu.roll(total, shift, 1)
        sc[...] = lax.rsqrt(total / (32.0 * V) + 1e-06)

        def member_grad(j):
            for mm in range(2):
                m = j * 2 + mm
                own = pf[m]
                pairs = jnp.zeros((VH, C), F32)
                for k in range(NK):
                    n, n_inv = match[k, m], inverse[m, k]
                    pairs = pairs + (own - pf[n]) * sc[pl.ds(k * MEMBERS + m, 1), :]
                    pairs = pairs + (own - pf[n_inv]) * sc[pl.ds(k * MEMBERS + n_inv, 1), :]
                truth = (own - tp[pr]) * sc[pl.ds(NK * MEMBERS + m, 1), :]
                gb[pr, j, mm] = (truth - pairs * (0.5 / NK)).astype(BF16)

        def member_pair(step, _):
            j = lax.rem(me + step, NM)
            member_grad(j)
            gradient_copy(pr, j, me).start()
            return 0

        lax.fori_loop(1, NM, member_pair, 0)
        member_grad(me)
        gr[pr, me] = gb[pr, me]

    def back_to_rows(pr):
        def gradients_in(step, _):
            source = lax.rem(me + step, NM)
            gradient_copy(pr, source, source).wait_recv()
            return 0

        lax.fori_loop(1, NM, gradients_in, 0)
        parts = []
        for t in range(8):
            rows = []
            for m in range(2):
                first, second = gr[pr, 2 * t, m].astype(F32), gr[pr, 2 * t + 1, m].astype(F32)
                rows.append(jnp.where(halves, first, half_turn(second)))
                rows.append(jnp.where(halves, half_turn(first), second))
            parts.append(jnp.concatenate(rows, axis=0).astype(BF16))
        back = dot_nt(jnp.concatenate(parts, axis=1), order()).astype(BF16)
        for m in range(2):
            for r in range(8):
                gn[m, pr * 8 + r] = back[m * VP:(m + 1) * VP, r * C:(r + 1) * C]

        def hidden_grad(rp, _):
            i = pr * 8 + rp * 2
            for m in range(2):
                dh = dot(wpt[...], pair(gn, m, i))
                for k in range(2):
                    gp[m, i + k + 1] = (dh[:, k * C:(k + 1) * C] * slope[m, i + k]).astype(BF16)
            return 0

        lax.fori_loop(0, 4, hidden_grad, 0)

    def wide(ref, i):
        return jnp.concatenate([ref[m, i + k] for m in range(2) for k in range(8)], axis=1)

    def conv_term(ro, pr):
        term = dot_nt(wide(gp, pr * 8 + 1), wide(x3, pr * 8 + ro))
        acc[ro][:, 0:KP] = term if pr == 0 else acc[ro][:, 0:KP] + term

    def proj_term(pr):
        term = dot_nt(wide(hidden, pr * 8), wide(gn, pr * 8))
        acc[0][:, KP:KP + VP] = term if pr == 0 else acc[0][:, KP:KP + VP] + term

    def core_copy(q):
        return remote(s1[q], r1[q], u_send.at[q], u_recv.at[q], member=me + 1 - 2 * core)

    def core_send(q):
        for c in range(NM // 2):
            base = c * 64 + (1 - core) * 32
            s1[q][c] = acc[q][pl.ds(pl.multiple_of(base, 32), 32), :].astype(BF16)
        core_copy(q).start()

    def sum_copy(place, source):
        return remote(
            s3.at[place], r3.at[source], w_send.at[place], w_recv.at[source],
            member=2 * lax.div(place, NB) + core, band=lax.rem(place, NB),
        )

    def sum_send():
        for q in range(3):
            core_copy(q).wait_recv()
        top = lax.broadcasted_iota(jnp.int32, (8, C), 0) < 4

        def pack(c, _):
            tiles = []
            for q in range(3):
                rows = pl.ds(pl.multiple_of(c * 64 + core * 32, 32), 32)
                value = acc[q][rows, :] + r1[q][c].astype(F32)
                tiles += [value[:, k * C:(k + 1) * C] for k in range(CHUNKS[q] // C)]
            tiles.append(jnp.zeros((32, C), F32))
            for g in range(4):
                parts = [tile[g * 8:(g + 1) * 8] for tile in tiles]
                turned = [pltpu.roll(part, 4, 0) for part in parts]
                first = [jnp.where(top, parts[k], turned[k + 1]) for k in range(0, 8, 2)]
                second = [jnp.where(top, turned[k], parts[k + 1]) for k in range(0, 8, 2)]
                s3[c * NB + 2 * g] = jnp.concatenate(first, axis=0).astype(BF16)
                s3[c * NB + 2 * g + 1] = jnp.concatenate(second, axis=0).astype(BF16)
            return 0

        lax.fori_loop(0, NM // 2, pack, 0)
        pl.semaphore_wait(ready, NB - 1)

        def send(step, _):
            sum_copy(lax.rem(spot + step, GROUP), spot).start()
            return 0

        lax.fori_loop(1, GROUP, send, 0)

    lax.fori_loop(1, 4, forward, 0)
    truth_patches()
    gp_zero = jnp.zeros((H, C), BF16)
    for m in range(2):
        gp[m, 0] = gp_zero
        gp[m, R + 1] = gp_zero
    acc[0][:, KP:] = jnp.zeros((H, 128), F32)
    halo_rows()
    forward(0, 0)
    predict(0)
    lax.fori_loop(4, 8, forward, 0)
    predict(1)
    to_scalars.wait()
    score(0)
    slopes(0)
    score(1)
    slopes(1)
    back_to_rows(0)
    proj_term(0)
    for ro in range(3):
        conv_term(ro, 0)
    back_to_rows(1)
    proj_term(1)
    conv_term(0, 1)
    core_send(0)
    conv_term(1, 1)
    core_send(1)
    conv_term(2, 1)
    core_send(2)

    def fold(d):
        def spread(a):
            return (
                jnp.where(lanes[0:a.shape[0]] == C - 1, 0.0, pltpu.roll(a, C - 1, 1)),
                jnp.where(lanes[0:a.shape[0]] == 0, 0.0, pltpu.roll(a, 1, 1)),
            )
        body = spread(d[0:80])[0] + d[80:160] + spread(d[160:240])[1]
        last = spread(d[240:248])[0] + pltpu.roll(d[240:248], 4, 0) + spread(d[248:256])[1]
        return jnp.concatenate([body, last], axis=0)

    for side, ro, row in ((0, 0, 1), (1, 2, R)):
        rows = jnp.concatenate([gp[0, row], gp[1, row]], axis=1)
        d = dot(wt[:, ro * H:(ro + 1) * H], rows)
        for m in range(2):
            edge = jnp.concatenate([fold(d[:, m * C:(m + 1) * C]), jnp.zeros((VP - VQ, C), F32)], axis=0)
            hsb[side, m] = edge.astype(BF16)

    def out_halo(side):
        to = band - 1 if side == 0 else band + 1
        return remote(hsb.at[side], hrb.at[1 - side], o_send.at[side], o_recv.at[1 - side], band=to)

    pl.when(band > 0)(lambda: out_halo(0).start())
    pl.when(band < NB - 1)(lambda: out_halo(1).start())

    def input_grad(m, low, high):
        def step(rp, _):
            i = rp * 2
            rows = jnp.concatenate([pair(gp, m, i + 2 - ro) for ro in range(3)], axis=0)
            d = dot(wt[...], rows)
            for k in range(2):
                value = fold(d[:, k * C:(k + 1) * C]) + gn[m, i + k].astype(F32)[0:VQ]
                of[m, pl.ds(i + k, VQ, stride=R), :] = value
            return 0

        lax.fori_loop(low, high, step, 0)

    sum_send()
    input_grad(0, 0, 8)
    input_grad(1, 0, 8)

    def out_halo_in(side, row):
        remote(hsb.at[1 - side], hrb.at[side], o_send.at[1 - side], o_recv.at[side], band=band).wait_recv()
        for m in range(2):
            of[m, pl.ds(row, VQ, stride=R), :] += hrb[side, m].astype(F32)[0:VQ]

    pl.when(band > 0)(lambda: out_halo_in(0, 0))
    pl.when(band < NB - 1)(lambda: out_halo_in(1, R - 1))

    def write(c, _):
        for m in range(2):
            value = of[m, pl.ds(pl.multiple_of(c * 192, 192), 192), :]
            out[m, pl.ds(c * 12, 12)] = value.reshape(12, R, C).astype(BF16)
        return 0

    lax.fori_loop(0, V // 12, write, 0)

    def sum_take(step, total):
        source = lax.rem(spot + GROUP - step, GROUP)
        sum_copy(source, source).wait_recv()
        return total + r3[source].astype(F32)

    total = lax.fori_loop(1, GROUP, sum_take, s3[spot].astype(F32))
    sums[...] = total * (1.0 / (MEMBERS * NB * R * C) ** 0.5)

    pl.when(band > 0)(lambda: halo(0).wait_send())
    pl.when(band < NB - 1)(lambda: halo(1).wait_send())
    for q in range(3):
        core_copy(q).wait_send()

    def sums_sent(step, _):
        sum_copy(lax.rem(spot + step, GROUP), spot).wait_send()
        return 0

    lax.fori_loop(1, GROUP, sums_sent, 0)
    pl.when(band > 0)(lambda: out_halo(0).wait_send())
    pl.when(band < NB - 1)(lambda: out_halo(1).wait_send())

    def sent(step, _):
        j = lax.rem(me + step, NM)
        for pr in range(2):
            predicted_copy(pr, j, me).wait_send()
            gradient_copy(pr, j, me).wait_send()
        return 0

    lax.fori_loop(1, NM, sent, 0)


def finish(grads, sums, out, conv, proj):
    out[...] = grads[...]
    wide = jnp.concatenate([sums[k * 4:(k + 1) * 4, :] for k in range(7)], axis=1)
    parts = []
    for base in (0, 384, 640):
        for co in range(3):
            parts += [wide[:, base + co * 80:base + (co + 1) * 80], wide[:, base + 240 + co * 4:base + 244 + co * 4]]
    conv[...] = jnp.concatenate(parts, axis=1)
    proj[...] = wide[:, KP:KP + V]


def on_device(states, noise_field, target, w_conv, w_proj, matchings):
    vmem = pl.BlockSpec(memory_space=pltpu.VMEM)
    smem = pl.BlockSpec(memory_space=pltpu.SMEM)
    D = pltpu.SemaphoreType.DMA
    S = pltpu.VMEM
    hbm = pl.BlockSpec(memory_space=pl.ANY)
    scratch = [
        S(states.shape, BF16), S(noise_field.shape, F32), S(target.shape, BF16), S((9 * V, H), BF16), S((V, H), BF16),
        S((8, 8 * C, C), BF16), S((MEMBERS, C), jnp.int32), pltpu.SMEM((MEMBERS, C), jnp.int32), S((9 * V, H), F32), D((7,)),
        S((2, VP * R, C), F32), S((2, R + 2, KP, C), BF16), S((2, 2, VP, C), BF16), S((2, 2, VP, C), BF16),
        S((H, 3 * KP), BF16), S((KP, 3 * H), BF16), S((VP, H), BF16), S((H, VP), BF16),
        S((2, R, H, C), BF16), S((2, R, H, C), F32), S((4, 2 * VP, 2 * C), BF16),
        S((2, NM, 2, VH, C), BF16), S((2, NM, 2, VH, C), BF16), S((MEMBERS, VH, C), F32),
        S((VP * R, C), F32), S((2, VH, C), F32), S(((NK + 1) * MEMBERS * 8, C), F32), S(((NK + 1) * MEMBERS, C), F32),
        S((2, NM, 2, VH, C), BF16), S((2, NM, 2, VH, C), BF16), S((2, R, VP, C), BF16),
        S((2, R + 2, H, C), BF16), S((2, VP * R, C), F32),
        S((2, 2, VP, C), BF16), S((2, 2, VP, C), BF16),
        *[S((H, w), F32) for w in CHUNKS],
        *[S((8, 32, w), BF16) for _ in range(2) for w in CHUNKS],
        S((GROUP, 32, C), BF16), S((GROUP, 32, C), BF16),
        D((2,)), D((2,)), D((2, NM)), D((2, NM)), D((2, NM)), D((2, NM)), D((2,)), D((2,)),
        D((3,)), D((3,)), D((GROUP,)), D((GROUP,)), pltpu.SemaphoreType.REGULAR,
    ]
    grad_states, sums = pl.pallas_call(
        kernel,
        out_shape=(
            jax.ShapeDtypeStruct(states.shape, BF16),
            jax.ShapeDtypeStruct((32, C), F32),
        ),
        in_specs=[hbm] * 6 + [smem, vmem],
        out_specs=(vmem, vmem),
        scratch_shapes=scratch,
        compiler_params=pltpu.CompilerParams(
            collective_id=0, has_side_effects=True, vmem_limit_bytes=60 * 1024 * 1024
        ),
    )(
        states, noise_field, target, w_conv.T, w_proj, jnp.asarray(patch_order()), matchings, matchings,
    )
    grad_states, grad_conv, grad_proj = pl.pallas_call(
        finish,
        out_shape=(
            jax.ShapeDtypeStruct(states.shape, BF16),
            jax.ShapeDtypeStruct((4, 9 * V), F32),
            jax.ShapeDtypeStruct((4, V), F32),
        ),
        in_specs=[vmem] * 2,
        out_specs=(vmem,) * 3,
    )(grad_states, sums)
    return grad_states, grad_conv, grad_proj.T


def solution(mesh):
    return jax.shard_map(
        on_device,
        mesh=mesh,
        in_specs=(
            P("member", None, "band", None),
            P("member", None, "band", None),
            P(None, "band", None),
            P(),
            P(),
            P(),
        ),
        out_specs=(
            P("member", None, "band", None),
            P(("member", "band"), None),
            P(None, ("member", "band")),
        ),
        check_vma=False,
    )
```
